256 devices in a mesh: pipe: 8 (over z), dp: 4 (over x), expert: 8 (over y, core).
Axes of the slice: x: 4, y: 4, z: 8, core: 2. Of those that a mesh axis runs over, the one named last changes fastest.
Arguments:
- handoff: bfloat16 [8, 1024, 3072], P('pipe', ('dp', 'expert')), may hold values from -6 to 6
- expert_ids: int32 [8, 1024, 4], P('pipe', ('dp', 'expert')), may hold values from 0 to 7, all different within a row; in each aligned block of 32 rows (0 to 31, 32 to 63, ..., all dimensions but the last counted through in order) at most 24 rows name the same one
- gates: bfloat16 [8, 1024, 4], P('pipe', ('dp', 'expert')), may hold values from 0.049804688 to 0.59765625
- down_weight: bfloat16 [8, 8, 5632, 3072], P('pipe', 'expert', 'dp'), may hold values from -0.078125 to 0.078125
- hidden: bfloat16 [8, 8, 768, 5632], P('pipe', 'expert', None, 'dp'), may hold values from -0.29882812 to 0.29882812
Outputs:
- hidden_grad: bfloat16 [8, 8, 768, 5632], P('pipe', 'expert', None, 'dp')
- gate_grad: float32 [8, 1024, 4], P('pipe', ('dp', 'expert'))
The draws below stay inside these ranges and needn't reach their ends.
Inputs may be any that keep to these rules, and one draw needn't show every extreme that they name: `expert_ids`: each token names 4 distinct experts. Among the 32 tokens of one device (aligned blocks) no expert is named more than 24 times, and in every draw some device names some expert exactly 24 times.
All inputs are finite; a program needn't handle non-finite values.
Results may differ from the reference program's by a relative error of at most 0.001.
Values may be sent and summed in bfloat16 or wider, within the bound.
No kernel may reach another device: no remote copies, remote signals or barrier semaphores. Data moves between devices by JAX's collectives and lax.ppermute only.
A program may use at most 64 MiB of HBM per device.

```python
import math
import jax
import jax.numpy as jnp
import numpy as np
from jax import lax

D = 3072
FFW = 5632
EXPERTS = 8
TOP = 4
TOK_DEV = 32
CAP = 24
SECTIONS = 8
TOKENS = 1024
SLOTS = 768


def steps_of(rng, shape, shards, smallest, high):
    def one(dim, parts):
        heights = jax.random.uniform(jax.random.fold_in(jax.random.fold_in(rng, 6), dim), (parts,), jnp.float32, smallest / len(shards), high / len(shards))
        return jnp.repeat(jnp.exp(heights), shape[dim] // parts).reshape((-1,) + (1,) * (len(shape) - dim - 1))

    loudness = one(*shards[0])
    for cut in shards[1:]:
        loudness = loudness * one(*cut)
    return loudness


def assign_block(rng, own, number, rows, number_of, top, most, slope):
    ranking = jax.random.permutation(rng, number_of)
    crowded, usual = portions_of(number_of, rows * top, most, slope, True), portions_of(number_of, rows * top, most, slope, False)
    places = jnp.arange(number_of)

    def named(tallies, offset_by):
        used = int((tallies > 0).sum())
        fixed = max(1, used // 4)
        shifted = fixed + (places - fixed + offset_by * (used - fixed)) % max(1, number_of - fixed)
        return jnp.zeros((number_of,), jnp.int32).at[ranking[jnp.where(places < fixed, places, shifted)]].set(jnp.asarray(tallies, jnp.int32))

    tallies = jnp.where(number % 4 == 0, named(crowded, number // 4), named(usual, number - number // 4 - 1))
    mixed = jax.random.permutation(jax.random.fold_in(own, 3), number_of)
    donor, taker = mixed[0:number_of // 2 * 2:2], mixed[1:number_of // 2 * 2:2]
    margin = jnp.minimum(tallies[donor] - 1, most - tallies[taker]) // 2
    margin = jnp.where((donor == ranking[0]) | (taker == ranking[0]) | (tallies[taker] == 0), 0, jnp.maximum(margin, 0))
    shifted = jax.random.randint(jax.random.fold_in(own, 4), (number_of // 2,), 0, 1 << 20) % (margin + 1)
    tallies = tallies.at[donor].add(-shifted).at[taker].add(shifted)
    labels = jnp.searchsorted(jnp.cumsum(tallies), jnp.arange(rows * top), side="right").astype(jnp.int32)
    table = labels.reshape(top, rows).T
    table = table[jax.random.permutation(jax.random.fold_in(own, 1), rows)]
    offset_by = jax.random.randint(jax.random.fold_in(own, 2), (rows, 1), 0, top)
    return jnp.take_along_axis(table, (jnp.arange(top)[None, :] + offset_by) % top, axis=1)


def portions_of(count, total, most, slope, full):
    loads = [(1 << 20) // math.isqrt(rank ** slope) + 1 for rank in range(1, count + 1)]
    largest = most if full else min(most, max(-(-total // count), total * loads[0] // sum(loads)))
    least = 1 if total - largest >= count - 1 else 0
    counts, rest = [largest] + [least] * (count - 1), total - largest - least * (count - 1)
    while rest > 0:
        candidates = [i for i in range(1, count) if counts[i] < largest] or [i for i in range(1, count) if counts[i] < most]
        mass, remaining = sum([loads[i] for i in candidates]), rest
        for i in candidates:
            more = min(most - counts[i], max(1, remaining * loads[i] // mass), rest)
            counts[i] = counts[i] + more
            rest = rest - more
    return np.array(counts)


def bell_draw(key, shape, deviation, reach, shards=(), kind=jnp.bfloat16):
    array = deviation * jax.random.normal(key, shape, jnp.float32)
    if shards:
        array = array * steps_of(key, shape, shards, -0.22, 0.18)
    return jnp.clip(array, -reach, reach).astype(kind)


def setup_inputs(seed: int = 0) -> dict:
    seeds = jax.random.split(jax.random.key(seed), 6)
    handoff = bell_draw(seeds[0], (SECTIONS, TOKENS, D), 1.0, 6.0, ((0, 8), (1, 32)))
    expert_ids_keys = jax.random.split(jax.random.fold_in(seeds[1], 1), SECTIONS * TOKENS // TOK_DEV)
    expert_ids_turns = jax.random.permutation(jax.random.fold_in(seeds[1], 3), SECTIONS * TOKENS // TOK_DEV)
    expert_ids = jax.vmap(lambda own, number: assign_block(jax.random.fold_in(seeds[1], 2), own, number, TOK_DEV, EXPERTS, TOP, CAP, 2))(expert_ids_keys, expert_ids_turns).reshape((SECTIONS, TOKENS, TOP))
    gates = jnp.clip(0.049804688 + 0.54785156 * jax.random.uniform(seeds[2], (SECTIONS, TOKENS, TOP), jnp.float32) ** steps_of(seeds[2], (SECTIONS, TOKENS, TOP), ((0, 8), (1, 32)), -0.2, 0.2), 0.049804688, 0.59765625).astype(jnp.bfloat16)
    down_weight = bell_draw(seeds[3], (SECTIONS, EXPERTS, FFW, D), FFW ** -0.5, 0.078125, ((0, 8), (1, 8), (2, 4)))
    hidden = bell_draw(seeds[4], (SECTIONS, EXPERTS, SLOTS, FFW), 0.05, 0.29882812, ((0, 8), (1, 8), (3, 4)))
    return dict(handoff=handoff, expert_ids=expert_ids, gates=gates, down_weight=down_weight, hidden=hidden)


def slot_index(route_blocks):
    onehot = (route_blocks[..., None] == jnp.arange(EXPERTS, dtype=jnp.int32)).astype(jnp.int32)
    before = jnp.cumsum(onehot, axis=-2) - onehot
    return jnp.sum(before * onehot, axis=-1).astype(jnp.int32)


def one_expert(operands):
    grad_rows, gate_rows, weight, saved_rows = operands
    product = jnp.dot(grad_rows, weight.T, preferred_element_type=jnp.float32)
    hidden_grad = (gate_rows.astype(jnp.float32)[:, None] * product).astype(jnp.bfloat16)
    return hidden_grad, jnp.sum(saved_rows.astype(jnp.float32) * product, axis=1)


def reference(handoff, expert_ids, gates, down_weight, hidden):
    incoming = jnp.roll(handoff, -1, axis=0)
    blocks = TOKENS // TOK_DEV
    per_block = expert_ids.reshape(SECTIONS, blocks, TOK_DEV * TOP)
    block_start = (jnp.arange(blocks, dtype=jnp.int32) * CAP)[None, :, None]
    columns = (block_start + slot_index(per_block)).reshape(SECTIONS, TOKENS * TOP).astype(jnp.int32)
    routes = expert_ids.reshape(SECTIONS, TOKENS * TOP)
    gate_flat = gates.reshape(SECTIONS, TOKENS * TOP)
    source = (jnp.arange(TOKENS * TOP, dtype=jnp.int32) // TOP).astype(jnp.int32)

    def one_section(operands):
        tokens_in, route_row, column_row, gate_row, weight, saved_rows = operands
        grad_rows = jnp.zeros((EXPERTS, SLOTS, D), tokens_in.dtype).at[route_row, column_row].set(tokens_in[source])
        gate_rows = jnp.zeros((EXPERTS, SLOTS), gate_row.dtype).at[route_row, column_row].set(gate_row)
        hidden_grad, sums = lax.map(one_expert, (grad_rows, gate_rows, weight, saved_rows))
        return hidden_grad, sums[route_row, column_row].reshape(TOKENS, TOP)

    return lax.map(one_section, (incoming, routes, columns, gate_flat, down_weight, hidden))
```

```python
import functools

import jax
import jax.numpy as jnp
from jax import lax
from jax.experimental import pallas as pl
from jax.experimental.pallas import tpu as pltpu
from jax.sharding import PartitionSpec as P

EXPERTS = 8
TOP = 4
CAP = 24
ROWS = 32
META = 128
TILE = 256
OFFSETS = (0, -1, 1, 2)
AXES = ("pipe", "dp", "expert")
VMEM_LIMIT = 44 * 1024 * 1024
F32 = jnp.float32
BF16 = jnp.bfloat16


def moved(x, to):
    nz, nx, ne = (lax.axis_size(a) for a in AXES)
    ny = ne // 2

    def index(z, i, j, c):
        return ((z % nz) * nx + i % nx) * ne + (j % ny) * 2 + c

    pairs = [
        (index(z, i, j, c), index(*to(z, i, j, c)))
        for z in range(nz)
        for i in range(nx)
        for j in range(ny)
        for c in range(2)
    ]
    return lax.ppermute(x, AXES, pairs)


def first(k):
    return lambda z, i, j, c: (z, i + k, j, c) if c == 0 else (z, i, j + k, c)


def second(k):
    return lambda z, i, j, c: (z, i, j + k, c) if c == 0 else (z, i + k, j, c)


def other_core(z, i, j, c):
    return (z, i, j, 1 - c)


def previous_section(z, i, j, c):
    return (z - 1, i, j, c)


def rows(*parts):
    return jnp.concatenate(parts, axis=0)


def load_weight(weight, held, sems):
    units = held.shape[0]
    copies = []
    for n, at in enumerate(range(0, units, TILE)):
        size = min(TILE, units - at)
        span = pl.ds(at, size)
        copies.append(pltpu.make_async_copy(weight.at[span, :], held.at[span, :], sems.at[n]))
    for copy in copies:
        copy.start()
    return copies


def pack(expert, token_refs, packed, gates):
    lane = lax.broadcasted_iota(jnp.int32, (16, META), 1)
    line = lax.broadcasted_iota(jnp.int32, (16, META), 0)
    pick = ((line == 0) & (lane == expert)).astype(F32).astype(BF16)
    spread = (
        lax.broadcasted_iota(jnp.int32, (META, META), 0) == EXPERTS + expert
    ).astype(F32).astype(BF16)
    at = 0
    for ref in token_refs:
        count, width = ref.shape
        width = width - META
        height = count // ROWS * CAP
        meta = ref[:, width:]
        slot = lax.dot_general(pick, meta, (((1,), (1,)), ((), ())), preferred_element_type=F32)[0:1, :]
        block = lax.broadcasted_iota(jnp.int32, (1, count), 1) // ROWS
        target = jnp.where(slot >= 0.0, slot.astype(jnp.int32) + block * CAP, -1)
        chosen = (
            lax.broadcasted_iota(jnp.int32, (height, count), 0) == target
        ).astype(F32).astype(BF16)
        for start in range(0, width, 512):
            packed[at : at + height, start : start + 512] = jnp.dot(
                chosen, ref[:, start : start + 512], preferred_element_type=F32
            ).astype(BF16)
        own = jnp.dot(chosen, meta, preferred_element_type=F32).astype(BF16)
        gates[at : at + height, :] = jnp.dot(own, spread, preferred_element_type=F32)
        at += height


def multiply(packed, held, copies, out):
    units = held.shape[0]
    for n, at in enumerate(range(0, units, TILE)):
        size = min(TILE, units - at)
        copies[n].wait()
        out[:, at : at + size] = lax.dot_general(
            packed[...],
            held[at : at + size, :],
            (((1,), (1,)), ((), ())),
            preferred_element_type=F32,
        )


def products_kernel(count, *refs):
    place = refs[0]
    tokens = refs[1 : 1 + count]
    weight, out, gates, held, packed, sems = refs[1 + count :]
    copies = load_weight(weight, held, sems)
    pack(place[3], tokens, packed, gates)
    multiply(packed, held, copies, out)


def smem():
    return pl.BlockSpec(memory_space=pltpu.SMEM)


def vmem():
    return pl.BlockSpec(memory_space=pltpu.VMEM)


def scratch(units, width, height):
    return [
        pltpu.VMEM((units, width), BF16),
        pltpu.VMEM((height, width), BF16),
        pltpu.SemaphoreType.DMA((pl.cdiv(units, TILE),)),
    ]


def cost(height, units, width):
    return pl.CostEstimate(
        flops=2 * height * units * width,
        bytes_accessed=2 * units * width + 4 * height * units,
        transcendentals=0,
    )


def products_of(place, tokens, weight):
    units, width = weight.shape
    height = sum(t.shape[0] for t in tokens) // ROWS * CAP
    return pl.pallas_call(
        functools.partial(products_kernel, len(tokens)),
        out_shape=(
            jax.ShapeDtypeStruct((height, units), F32),
            jax.ShapeDtypeStruct((height, META), F32),
        ),
        in_specs=[smem()] + [vmem()] * len(tokens) + [pl.BlockSpec(memory_space=pl.ANY)],
        out_specs=(vmem(), vmem()),
        scratch_shapes=scratch(units, width, height),
        compiler_params=pltpu.CompilerParams(vmem_limit_bytes=VMEM_LIMIT),
        cost_estimate=cost(height, units, width),
    )(place, *tokens, weight)


def last_kernel(
    place, mine, theirs, weight, hidden, near, near_gates, mid, mid_gates, out, sums,
    held, packed, sems, far, far_gates,
):
    copies = load_weight(weight, held, sems)
    pack(place[3], (mine, theirs), packed, far_gates)
    multiply(packed, held, copies, far)
    units = held.shape[0]
    core = place[2]
    diagonal = lax.broadcasted_iota(jnp.int32, (CAP, META), 0) == lax.broadcasted_iota(
        jnp.int32, (CAP, META), 1
    )

    def part(kind, along, across):
        which = jnp.where(core == kind, 0, 1)
        a = OFFSETS.index(along)
        if across == 0:
            return near, near_gates, (which * 4 + a) * CAP
        if across == 2:
            return far, far_gates, (which * 4 + a) * CAP
        return mid, mid_gates, (which * 8 + (0 if across == -1 else 4) + a) * CAP

    for i in OFFSETS:
        for j in OFFSETS:
            chip = ((place[0] + (i + 4)) % 4) * 4 + (place[1] + (j + 4)) % 4
            at = pl.multiple_of(chip * (2 * CAP), 16)
            pieces = [part(0, i, j), part(1, j, i)]
            spans = [pl.ds(pl.multiple_of(p[2], 8), CAP) for p in pieces]
            scale = jnp.concatenate([p[1][s, :] for p, s in zip(pieces, spans)], axis=0)
            total = jnp.zeros((2 * CAP, META), F32)
            for col in range(0, units, META):
                value = jnp.concatenate(
                    [p[0][s, col : col + META] for p, s in zip(pieces, spans)], axis=0
                )
                out[pl.ds(at, 2 * CAP), col : col + META] = (scale * value).astype(BF16)
                saved = hidden[pl.ds(at, 2 * CAP), col : col + META].astype(F32)
                total = total + saved * value
            total = jnp.sum(total, axis=1, keepdims=True)
            for kind in range(2):
                line = jnp.sum(
                    jnp.where(diagonal, total[kind * CAP : (kind + 1) * CAP], 0.0),
                    axis=0,
                    keepdims=True,
                )
                sums[pl.ds(chip * 2 + kind, 1), :] = line


def last_of(place, mine, theirs, weight, hidden, near, near_gates, mid, mid_gates):
    units, width = weight.shape
    height = 2 * mine.shape[0] // ROWS * CAP
    return pl.pallas_call(
        last_kernel,
        out_shape=(
            jax.ShapeDtypeStruct(hidden.shape, BF16),
            jax.ShapeDtypeStruct((hidden.shape[0] // CAP, META), F32),
        ),
        in_specs=[smem(), vmem(), vmem(), pl.BlockSpec(memory_space=pl.ANY)] + [vmem()] * 5,
        out_specs=(vmem(), vmem()),
        scratch_shapes=scratch(units, width, height)
        + [pltpu.VMEM((height, units), F32), pltpu.VMEM((height, META), F32)],
        compiler_params=pltpu.CompilerParams(vmem_limit_bytes=VMEM_LIMIT),
        cost_estimate=cost(height, units, width),
    )(place, mine, theirs, weight, hidden, near, near_gates, mid, mid_gates)


def gather_kernel(totals, ids, slots, out):
    quarter = totals.shape[0] // 4
    total = totals[0:quarter, :]
    for n in range(1, 4):
        total = total + totals[n * quarter : (n + 1) * quarter, :]
    tokens = ids.shape[0]
    lane = lax.broadcasted_iota(jnp.int32, (tokens, META), 1)
    place = lax.broadcasted_iota(jnp.int32, (tokens, TOP), 1)
    result = jnp.zeros((tokens, TOP), F32)
    for k in range(TOP):
        expert = ids[:, k : k + 1]
        line = jnp.zeros((tokens, META), F32)
        for e in range(EXPERTS):
            line = jnp.where(expert == e, total[e : e + 1, :], line)
        value = jnp.sum(jnp.where(lane == slots[:, k : k + 1], line, 0.0), axis=1, keepdims=True)
        result = jnp.where(place == k, value, result)
    out[...] = result


def on_device(handoff, expert_ids, gates, down_weight, hidden):
    dp, expert = lax.axis_index("dp"), lax.axis_index("expert")
    place = jnp.stack([dp, expert // 2, expert % 2, expert]).astype(jnp.int32)
    ids = expert_ids[0]
    weight = down_weight[0, 0]
    incoming = moved(handoff[0], previous_section)
    named = ids[:, :, None] == jnp.arange(EXPERTS, dtype=jnp.int32)
    any_named = named.any(axis=1).astype(jnp.int32)
    before = jnp.cumsum(any_named, axis=0) - any_named
    slot_map = jnp.where(any_named > 0, before, -1)
    gate_map = jnp.sum(jnp.where(named, gates[0][:, :, None].astype(F32), 0.0), axis=1)
    slots = jnp.sum(jnp.where(named, before[:, None, :], 0), axis=2)
    meta = jnp.concatenate([slot_map.astype(F32), gate_map], axis=1).astype(BF16)
    meta = jnp.pad(meta, ((0, 0), (0, META - 2 * EXPERTS)))
    own = jnp.concatenate([incoming, meta], axis=1)

    near = rows(own, *[moved(own, first(k)) for k in (1, 3, 2)])
    low, high = moved(near, second(1)), moved(near, second(3))
    half = near.shape[0] // 2
    far = rows(moved(high[:half], second(3)), moved(low[half:], second(1)))
    mid = rows(low, high)
    near_other = moved(near, other_core)
    mid_other = moved(mid, other_core)
    far_other = moved(far, other_core)
    near_products, near_gates = products_of(place, (near, near_other), weight)
    mid_products, mid_gates = products_of(place, (mid, mid_other), weight)
    hidden_grad, sums = last_of(
        place, far, far_other, weight, hidden[0, 0], near_products, near_gates, mid_products, mid_gates
    )
    totals = lax.all_to_all(sums, ("dp", "expert"), split_axis=0, concat_axis=0, tiled=True)
    gate_grad = pl.pallas_call(
        gather_kernel,
        out_shape=jax.ShapeDtypeStruct(ids.shape, F32),
        in_specs=[vmem()] * 3,
        out_specs=vmem(),
    )(totals, ids, slots)
    return (hidden_grad[None, None], gate_grad[None])


def solution(mesh):
    return jax.shard_map(
        on_device,
        mesh=mesh,
        in_specs=(
            P("pipe", ("dp", "expert"), None),
            P("pipe", ("dp", "expert"), None),
            P("pipe", ("dp", "expert"), None),
            P("pipe", "expert", "dp", None),
            P("pipe", "expert", None, "dp"),
        ),
        out_specs=(P("pipe", "expert", None, "dp"), P("pipe", ("dp", "expert"), None)),
        check_vma=False,
    )
```

```python
import jax
import jax.numpy as jnp
from jax import lax
from jax.experimental import pallas as pl
from jax.experimental.pallas import tpu as pltpu
from jax.sharding import PartitionSpec as P

EXPERTS = 8
TOP = 4
CAP = 24
ROWS = 32
META = 128
TILE = 256
OFFSETS = (0, -1, 1, 2)
HALVES = tuple((0, 2, j) for j in (0, -1, 1)) + tuple((1, i, 2) for i in (0, -1, 1))
AXES = ("pipe", "dp", "expert")
VMEM_LIMIT = 20
F32 = jnp.float32
BF16 = jnp.bfloat16


def moved(x, to):
    nz, nx, ne = (lax.axis_size(a) for a in AXES)
    ny = ne // 2

    def index(z, i, j, c):
        return ((z % nz) * nx + i % nx) * ne + (j % ny) * 2 + c

    pairs = [
        (index(z, i, j, c), index(*to(z, i, j, c)))
        for z in range(nz)
        for i in range(nx)
        for j in range(ny)
        for c in range(2)
    ]
    return lax.ppermute(x, AXES, pairs)


def first(k):
    return lambda z, i, j, c: (z, i + k, j, c) if c == 0 else (z, i, j + k, c)


def second(k):
    return lambda z, i, j, c: (z, i, j + k, c) if c == 0 else (z, i + k, j, c)


def other_core(z, i, j, c):
    return (z, i, j, 1 - c)


def previous_section(z, i, j, c):
    return (z - 1, i, j, c)


def rows(*parts):
    return jnp.concatenate(parts, axis=0)


def pack(expert, token_refs, packed, gates):
    lane = lax.broadcasted_iota(jnp.int32, (16, META), 1)
    line = lax.broadcasted_iota(jnp.int32, (16, META), 0)
    pick = ((line == 0) & (lane == expert)).astype(F32).astype(BF16)
    spread = (
        lax.broadcasted_iota(jnp.int32, (META, META), 0) == EXPERTS + expert
    ).astype(F32).astype(BF16)
    at = 0
    for ref in token_refs:
        count, width = ref.shape
        width = width - META
        height = count // ROWS * CAP
        meta = ref[:, width:]
        slot = lax.dot_general(pick, meta, (((1,), (1,)), ((), ())), preferred_element_type=F32)[0:1, :]
        block = lax.broadcasted_iota(jnp.int32, (1, count), 1) // ROWS
        target = jnp.where(slot >= 0.0, slot.astype(jnp.int32) + block * CAP, -1)
        chosen = (
            lax.broadcasted_iota(jnp.int32, (height, count), 0) == target
        ).astype(F32).astype(BF16)
        for start in range(0, width, 512):
            packed[at : at + height, start : start + 512] = jnp.dot(
                chosen, ref[:, start : start + 512], preferred_element_type=F32
            ).astype(BF16)
        own = jnp.dot(chosen, meta, preferred_element_type=F32).astype(BF16)
        gates[at : at + height, :] = jnp.dot(own, spread, preferred_element_type=F32)
        at += height


def multiply(packed, turned, out):
    units = turned.shape[1]
    for at in range(0, units, TILE):
        size = min(TILE, units - at)
        out[:, at : at + size] = jnp.dot(
            packed[...], turned[:, at : at + size], preferred_element_type=F32
        )


def smem():
    return pl.BlockSpec(memory_space=pltpu.SMEM)


def vmem():
    return pl.BlockSpec(memory_space=pltpu.VMEM)


def anywhere():
    return pl.BlockSpec(memory_space=pl.ANY)


def params(mebibytes=VMEM_LIMIT):
    return pltpu.CompilerParams(vmem_limit_bytes=mebibytes << 20)


def cost(height, units, width):
    return pl.CostEstimate(
        flops=2 * height * units * width,
        bytes_accessed=2 * units * width + 4 * height * units,
        transcendentals=0,
    )


def meta_kernel(place, ids, gates, meta, lines, spot):
    for n in range(4):
        spot[n] = place[n]
    tokens = ids.shape[1]
    expert = lax.broadcasted_iota(jnp.int32, (EXPERTS, tokens), 0)
    named = [ids[k : k + 1, :] == expert for k in range(TOP)]
    some = jnp.zeros((EXPERTS, tokens), F32)
    gate = jnp.zeros((EXPERTS, tokens), F32)
    weights = gates[...].astype(F32)
    for k in range(TOP):
        some = jnp.where(named[k], 1.0, some)
        gate = jnp.where(named[k], weights[k : k + 1, :], gate)
    row = lax.broadcasted_iota(jnp.int32, (tokens, tokens), 0)
    col = lax.broadcasted_iota(jnp.int32, (tokens, tokens), 1)
    earlier = (row < col).astype(F32).astype(BF16)
    before = jnp.dot(some.astype(BF16), earlier, preferred_element_type=F32)
    slot = jnp.where(some > 0.0, before, -1.0)
    lines[...] = jnp.zeros(lines.shape, jnp.int32)
    for k in range(TOP):
        own = jnp.sum(jnp.where(named[k], before, 0.0), axis=0, keepdims=True)
        lines[0:1, k * tokens : (k + 1) * tokens] = own.astype(jnp.int32)
        lines[1:2, k * tokens : (k + 1) * tokens] = ids[k : k + 1, :]
    table = jnp.concatenate(
        [slot, gate, jnp.zeros((META - 2 * EXPERTS, tokens), F32)], axis=0
    ).astype(BF16)
    unit = (row == col).astype(F32).astype(BF16)
    meta[...] = lax.dot_general(
        unit, table, (((1,), (1,)), ((), ())), preferred_element_type=F32
    ).astype(BF16)


def meta_of(place, ids, gates):
    return pl.pallas_call(
        meta_kernel,
        out_shape=(
            jax.ShapeDtypeStruct((ids.shape[1], META), BF16),
            jax.ShapeDtypeStruct((8, META), jnp.int32),
            jax.ShapeDtypeStruct((4,), jnp.int32),
        ),
        in_specs=[smem(), vmem(), vmem()],
        out_specs=(vmem(), vmem(), smem()),
        compiler_params=params(2),
    )(place, ids, gates)


def join_kernel(*refs):
    at = 0
    for ref in refs[:-1]:
        refs[-1][at : at + ref.shape[0], :] = ref[...]
        at += ref.shape[0]


def join(*parts):
    shape = (sum(p.shape[0] for p in parts), parts[0].shape[1])
    return pl.pallas_call(
        join_kernel,
        out_shape=pltpu.VMEM(shape, parts[0].dtype),
        in_specs=[vmem()] * len(parts),
        out_specs=vmem(),
        compiler_params=params(6),
    )(*parts)


def turn_kernel(place, weight, turned, held, sems):
    units, width = weight.shape
    copies = [
        pltpu.make_async_copy(
            weight.at[pl.ds(at, META), :], held.at[pl.ds(at, META), :], sems.at[at // META]
        )
        for at in range(0, units, META)
    ]
    for copy in copies:
        copy.start()
    for copy, at in zip(copies, range(0, units, META)):
        copy.wait()
        for col in range(0, width, 512):
            turned[col : col + 512, at : at + META] = held[at : at + META, col : col + 512].T


def turn(place, weight):
    units, width = weight.shape
    return pl.pallas_call(
        turn_kernel,
        out_shape=pltpu.VMEM((width, units), BF16),
        in_specs=[smem(), anywhere()],
        out_specs=vmem(),
        scratch_shapes=[
            pltpu.VMEM((units, width), BF16),
            pltpu.SemaphoreType.DMA((units // META,)),
        ],
        compiler_params=params(),
        cost_estimate=pl.CostEstimate(
            flops=0, bytes_accessed=4 * units * width, transcendentals=0
        ),
    )(place, pltpu.with_memory_space_constraint(weight, pltpu.HBM))


def near_kernel(place, mine, theirs, turned, out, gates, packed):
    pack(place[3], (mine, theirs), packed, gates)
    multiply(packed, turned, out)


def near_of(place, mine, theirs, turned):
    width, units = turned.shape
    height = 2 * mine.shape[0] // ROWS * CAP
    return pl.pallas_call(
        near_kernel,
        out_shape=(pltpu.VMEM((height, units), F32), pltpu.VMEM((height, META), F32)),
        in_specs=[smem()] + [vmem()] * 3,
        out_specs=(vmem(), vmem()),
        scratch_shapes=[pltpu.VMEM((height, width), BF16)],
        compiler_params=params(),
        cost_estimate=cost(height, units, width),
    )(place, mine, theirs, turned)


def chip_of(place, i, j):
    return ((place[0] + (i + 4)) % 4) * 4 + (place[1] + (j + 4)) % 4


def pair_rows(chip):
    return pl.ds(pl.multiple_of(chip * (2 * CAP), 16), 2 * CAP)


def block_rows(place, kind, group, along):
    which = jnp.where(place[2] == kind, 0, 1)
    return pl.ds(pl.multiple_of((which * group + along) * CAP, 8), CAP)


def finish(chip, pieces, saved, sums, write):
    diagonal = lax.broadcasted_iota(jnp.int32, (CAP, META), 0) == lax.broadcasted_iota(
        jnp.int32, (CAP, META), 1
    )
    scales = [None if p is None or p[1] is None else p[1][p[2], :] for p in pieces]
    totals = [jnp.zeros((CAP, META), F32) for _ in pieces]
    for col in range(0, saved.shape[1], META):
        span = slice(col, col + META)
        factor = saved[pair_rows(chip), span].astype(F32)
        scaled = []
        for kind, piece in enumerate(pieces):
            if piece is None:
                scaled.append(None)
                continue
            value = piece[0][piece[2], span]
            if scales[kind] is not None:
                totals[kind] += factor[kind * CAP : (kind + 1) * CAP] * value
                value = scales[kind] * value
            scaled.append(value)
        write(span, scaled)
    for kind, scale in enumerate(scales):
        if scale is not None:
            total = jnp.sum(totals[kind], axis=1, keepdims=True)
            sums[pl.ds(chip * 2 + kind, 1), :] = jnp.sum(
                jnp.where(diagonal, total, 0.0), axis=0, keepdims=True
            )


def staged(stage, slot):
    def write(span, scaled):
        stage[slot, :, span] = jnp.concatenate(scaled, axis=0).astype(BF16)

    return write


def mid_kernel(
    place, mine, theirs, turned, hidden, near, near_gates,
    grad, sums, halves, packed, mid, mid_gates, stage, sems,
):
    pack(place[3], (mine, theirs), packed, mid_gates)
    multiply(packed, turned, mid)

    def piece(kind, along, across):
        a = OFFSETS.index(along)
        if across == 0:
            return near, near_gates, block_rows(place, kind, 4, a)
        return mid, mid_gates, block_rows(place, kind, 8, (0 if across == -1 else 4) + a)

    copies = []
    for i in (0, -1, 1):
        for j in (0, -1, 1):
            chip, slot = chip_of(place, i, j), len(copies)
            finish(chip, (piece(0, i, j), piece(1, j, i)), hidden, sums, staged(stage, slot))
            copy = pltpu.make_async_copy(stage.at[slot], grad.at[pair_rows(chip), :], sems.at[slot])
            copy.start()
            copies.append(copy)
    for n, (kind, i, j) in enumerate(HALVES):
        def write(span, scaled, kind=kind, n=n):
            halves[n * CAP : (n + 1) * CAP, span] = scaled[kind]

        pieces = (piece(0, i, j), None) if kind == 0 else (None, piece(1, j, i))
        finish(chip_of(place, i, j), pieces, hidden, sums, write)
    for copy in copies:
        copy.wait()


def mid_of(place, mine, theirs, turned, hidden, near, near_gates):
    width, units = turned.shape
    height = 2 * mine.shape[0] // ROWS * CAP
    return pl.pallas_call(
        mid_kernel,
        out_shape=(
            jax.ShapeDtypeStruct(hidden.shape, BF16),
            pltpu.VMEM((hidden.shape[0] // CAP, META), F32),
            pltpu.VMEM((len(HALVES) * CAP, units), F32),
        ),
        in_specs=[smem()] + [vmem()] * 6,
        out_specs=(anywhere(), vmem(), vmem()),
        scratch_shapes=[
            pltpu.VMEM((height, width), BF16),
            pltpu.VMEM((height, units), F32),
            pltpu.VMEM((height, META), F32),
            pltpu.VMEM((9, 2 * CAP, units), BF16),
            pltpu.SemaphoreType.DMA((9,)),
        ],
        compiler_params=params(),
        cost_estimate=cost(height, units, width),
    )(place, mine, theirs, turned, hidden, near, near_gates)


def far_kernel(
    place, mine, theirs, turned, hidden, halves, early, _, grad, sums,
    packed, far, far_gates, stage, sems,
):
    sums[...] = early[...]
    pack(place[3], (mine, theirs), packed, far_gates)
    multiply(packed, turned, far)
    copies = []
    for i in OFFSETS:
        for j in OFFSETS:
            if i != 2 and j != 2:
                continue
            pieces = []
            for kind, along, across in ((0, i, j), (1, j, i)):
                if across == 2:
                    rows_of = block_rows(place, kind, 4, OFFSETS.index(along))
                    pieces.append((far, far_gates, rows_of))
                else:
                    n = HALVES.index((kind, i, j))
                    pieces.append((halves, None, pl.ds(n * CAP, CAP)))
            chip, slot = chip_of(place, i, j), len(copies)
            finish(chip, pieces, hidden, sums, staged(stage, slot))
            copy = pltpu.make_async_copy(stage.at[slot], grad.at[pair_rows(chip), :], sems.at[slot])
            copy.start()
            copies.append(copy)
    for copy in copies:
        copy.wait()


def far_of(place, mine, theirs, turned, hidden, halves, early, grad):
    width, units = turned.shape
    height = 2 * mine.shape[0] // ROWS * CAP
    return pl.pallas_call(
        far_kernel,
        out_shape=(
            jax.ShapeDtypeStruct(grad.shape, BF16),
            pltpu.VMEM(early.shape, F32),
        ),
        in_specs=[smem()] + [vmem()] * 6 + [anywhere()],
        out_specs=(anywhere(), vmem()),
        scratch_shapes=[
            pltpu.VMEM((height, width), BF16),
            pltpu.VMEM((height, units), F32),
            pltpu.VMEM((height, META), F32),
            pltpu.VMEM((7, 2 * CAP, units), BF16),
            pltpu.SemaphoreType.DMA((7,)),
        ],
        input_output_aliases={7: 0},
        compiler_params=params(),
        cost_estimate=cost(height, units, width),
    )(place, mine, theirs, turned, hidden, halves, early, grad)


def gather_kernel(totals, lines, out):
    quarter = totals.shape[0] // 4
    total = totals[0:quarter, :]
    for n in range(1, 4):
        total = total + totals[n * quarter : (n + 1) * quarter, :]
    pick = (lax.broadcasted_iota(jnp.int32, (META, META), 0) == lines[0:1, :]).astype(F32)
    line = jnp.dot(total, pick, precision=lax.Precision.HIGHEST, preferred_element_type=F32)
    chosen = lax.broadcasted_iota(jnp.int32, line.shape, 0) == lines[1:2, :]
    line = jnp.sum(jnp.where(chosen, line, 0.0), axis=0, keepdims=True)
    tokens = out.shape[1]
    for k in range(TOP):
        out[k : k + 1, :] = line[:, k * tokens : (k + 1) * tokens]


def on_device(handoff, expert_ids, gates, down_weight, hidden):
    dp, expert = lax.axis_index("dp"), lax.axis_index("expert")
    place = jnp.stack([dp, expert // 2, expert % 2, expert]).astype(jnp.int32)
    ids = expert_ids[0].T
    incoming = moved(handoff[0], previous_section)
    meta, lines, place = meta_of(place, ids, gates[0].T)
    own = jnp.concatenate([incoming, meta], axis=1)
    own, lines, place = lax.optimization_barrier((own, lines, place))

    ahead, back, across = [moved(own, first(k)) for k in (1, 3, 2)]
    ahead, back, across = lax.optimization_barrier((ahead, back, across))
    near = rows(own, ahead), rows(back, across)
    high = [moved(near[0], second(3)), None]
    low = [None, moved(near[1], second(1))]
    low[0] = moved(near[0], second(1))
    high[1] = moved(near[1], second(3))
    near = rows(*near)
    near, later = lax.optimization_barrier((near, place))
    turned = turn(later, down_weight[0, 0])
    near_other = moved(near, other_core)
    near_products, near_gates = near_of(place, near, near_other, turned)
    high[0], low[1], near_products, near_gates = lax.optimization_barrier(
        (high[0], low[1], near_products, near_gates)
    )
    far = moved(high[0], second(3)), moved(low[1], second(1))
    mid = join(*low, *high)
    mid_other = moved(mid, other_core)
    grad, sums, halves = mid_of(
        place, mid, mid_other, turned, hidden[0, 0], near_products, near_gates
    )
    far, grad, sums, halves = lax.optimization_barrier((far, grad, sums, halves))
    far = join(*far)
    far_other = moved(far, other_core)
    grad, sums = far_of(place, far, far_other, turned, hidden[0, 0], halves, sums, grad)
    totals = lax.all_to_all(sums, ("dp", "expert"), split_axis=0, concat_axis=0, tiled=True)
    gate_grad = pl.pallas_call(
        gather_kernel,
        out_shape=jax.ShapeDtypeStruct(ids.shape, F32),
        in_specs=[vmem()] * 2,
        out_specs=vmem(),
        compiler_params=params(2),
    )(totals, lines)
    return (grad[None, None], gate_grad.T[None])


def solution(mesh):
    return jax.shard_map(
        on_device,
        mesh=mesh,
        in_specs=(
            P("pipe", ("dp", "expert"), None),
            P("pipe", ("dp", "expert"), None),
            P("pipe", ("dp", "expert"), None),
            P("pipe", "expert", "dp", None),
            P("pipe", "expert", None, "dp"),
        ),
        out_specs=(P("pipe", "expert", None, "dp"), P("pipe", ("dp", "expert"), None)),
        check_vma=False,
    )
```

```python
import jax
import jax.numpy as jnp
from jax import lax
from jax.experimental import pallas as pl
from jax.experimental.pallas import tpu as pltpu
from jax.sharding import PartitionSpec as P

EXPERTS = 8
TOP = 4
CAP = 24
ROWS = 32
META = 128
TILE = 256
OFFSETS = (0, -1, 1, 2)
HALVES = tuple((0, 2, j) for j in (0, -1, 1)) + tuple((1, i, 2) for i in (0, -1, 1))
AXES = ("pipe", "dp", "expert")
VMEM_LIMIT = 20
F32 = jnp.float32
BF16 = jnp.bfloat16


def moved(x, to):
    nz, nx, ne = (lax.axis_size(a) for a in AXES)
    ny = ne // 2

    def index(z, i, j, c):
        return ((z % nz) * nx + i % nx) * ne + (j % ny) * 2 + c

    pairs = [
        (index(z, i, j, c), index(*to(z, i, j, c)))
        for z in range(nz)
        for i in range(nx)
        for j in range(ny)
        for c in range(2)
    ]
    return lax.ppermute(x, AXES, pairs)


def first(k):
    return lambda z, i, j, c: (z, i + k, j, c) if c == 0 else (z, i, j + k, c)


def second(k):
    return lambda z, i, j, c: (z, i, j + k, c) if c == 0 else (z, i + k, j, c)


def other_core(z, i, j, c):
    return (z, i, j, 1 - c)


def previous_section(z, i, j, c):
    return (z - 1, i, j, c)


def rows(*parts):
    return jnp.concatenate(parts, axis=0)


def pack(expert, token_refs, packed, gates):
    lane = lax.broadcasted_iota(jnp.int32, (16, META), 1)
    line = lax.broadcasted_iota(jnp.int32, (16, META), 0)
    pick = ((line == 0) & (lane == expert)).astype(F32).astype(BF16)
    spread = (
        lax.broadcasted_iota(jnp.int32, (META, META), 0) == EXPERTS + expert
    ).astype(F32).astype(BF16)
    at = 0
    for ref in token_refs:
        count, width = ref.shape
        width = width - META
        height = count // ROWS * CAP
        meta = ref[:, width:]
        slot = lax.dot_general(pick, meta, (((1,), (1,)), ((), ())), preferred_element_type=F32)[0:1, :]
        block = lax.broadcasted_iota(jnp.int32, (1, count), 1) // ROWS
        target = jnp.where(slot >= 0.0, slot.astype(jnp.int32) + block * CAP, -1)
        chosen = (
            lax.broadcasted_iota(jnp.int32, (height, count), 0) == target
        ).astype(F32).astype(BF16)
        for start in range(0, width, 512):
            packed[at : at + height, start : start + 512] = jnp.dot(
                chosen, ref[:, start : start + 512], preferred_element_type=F32
            ).astype(BF16)
        own = jnp.dot(chosen, meta, preferred_element_type=F32).astype(BF16)
        gates[at : at + height, :] = jnp.dot(own, spread, preferred_element_type=F32)
        at += height


def multiply(packed, turned, out):
    units = turned.shape[1]
    for at in range(0, units, TILE):
        size = min(TILE, units - at)
        out[:, at : at + size] = jnp.dot(
            packed[...], turned[:, at : at + size], preferred_element_type=F32
        )


def smem():
    return pl.BlockSpec(memory_space=pltpu.SMEM)


def vmem():
    return pl.BlockSpec(memory_space=pltpu.VMEM)


def anywhere():
    return pl.BlockSpec(memory_space=pl.ANY)


def params(mebibytes=VMEM_LIMIT):
    return pltpu.CompilerParams(vmem_limit_bytes=mebibytes << 20)


def small():
    return pl.CostEstimate(flops=1, bytes_accessed=1, transcendentals=0)


def meta_kernel(place, ids, gates, meta, lines, spot):
    for n in range(4):
        spot[n] = place[n]
    tokens = ids.shape[1]
    expert = lax.broadcasted_iota(jnp.int32, (EXPERTS, tokens), 0)
    named = [ids[k : k + 1, :] == expert for k in range(TOP)]
    some = jnp.zeros((EXPERTS, tokens), F32)
    gate = jnp.zeros((EXPERTS, tokens), F32)
    weights = gates[...].astype(F32)
    for k in range(TOP):
        some = jnp.where(named[k], 1.0, some)
        gate = jnp.where(named[k], weights[k : k + 1, :], gate)
    row = lax.broadcasted_iota(jnp.int32, (tokens, tokens), 0)
    col = lax.broadcasted_iota(jnp.int32, (tokens, tokens), 1)
    earlier = (row < col).astype(F32).astype(BF16)
    before = jnp.dot(some.astype(BF16), earlier, preferred_element_type=F32)
    slot = jnp.where(some > 0.0, before, -1.0)
    lines[...] = jnp.zeros(lines.shape, jnp.int32)
    for k in range(TOP):
        own = jnp.sum(jnp.where(named[k], before, 0.0), axis=0, keepdims=True)
        lines[0:1, k * tokens : (k + 1) * tokens] = own.astype(jnp.int32)
        lines[1:2, k * tokens : (k + 1) * tokens] = ids[k : k + 1, :]
    table = jnp.concatenate(
        [slot, gate, jnp.zeros((META - 2 * EXPERTS, tokens), F32)], axis=0
    ).astype(BF16)
    unit = (row == col).astype(F32).astype(BF16)
    meta[...] = lax.dot_general(
        unit, table, (((1,), (1,)), ((), ())), preferred_element_type=F32
    ).astype(BF16)


def meta_of(place, ids, gates):
    return pl.pallas_call(
        meta_kernel,
        out_shape=(
            jax.ShapeDtypeStruct((ids.shape[1], META), BF16),
            jax.ShapeDtypeStruct((8, META), jnp.int32),
            jax.ShapeDtypeStruct((4,), jnp.int32),
        ),
        in_specs=[smem(), vmem(), vmem()],
        out_specs=(vmem(), vmem(), smem()),
        compiler_params=params(2),
    )(place, ids, gates)


def join_kernel(*refs):
    at = 0
    for ref in refs[:-1]:
        refs[-1][at : at + ref.shape[0], :] = ref[...]
        at += ref.shape[0]


def join(*parts):
    shape = (sum(p.shape[0] for p in parts), parts[0].shape[1])
    return pl.pallas_call(
        join_kernel,
        out_shape=pltpu.VMEM(shape, parts[0].dtype),
        in_specs=[vmem()] * len(parts),
        out_specs=vmem(),
        compiler_params=params(6),
        cost_estimate=small(),
    )(*parts)


def halves_kernel(high, low, first_half, second_half):
    half = first_half.shape[0]
    first_half[...] = high[:half, :]
    second_half[...] = low[half:, :]


def halves_of(high, low):
    shape = (high.shape[0] // 2, high.shape[1])
    return pl.pallas_call(
        halves_kernel,
        out_shape=(pltpu.VMEM(shape, BF16), pltpu.VMEM(shape, BF16)),
        in_specs=[vmem()] * 2,
        out_specs=(vmem(), vmem()),
        compiler_params=params(6),
        cost_estimate=small(),
    )(high, low)


def far_block(place, n):
    which, a = divmod(n, 4)
    kind = place[2] if which == 0 else 1 - place[2]
    x = jnp.where(kind == 0, OFFSETS[a], 2)
    y = jnp.where(kind == 0, 2, OFFSETS[a])
    return kind, chip_of(place, x, y)


def turn_kernel(place, hidden, weight, turned, ahead, held, far, sems):
    units, width = weight.shape
    starts = range(0, units, TILE)
    spans = [pl.ds(at, min(TILE, units - at)) for at in starts]
    copies = [
        pltpu.make_async_copy(weight.at[span, :], held.at[span, :], sems.at[n])
        for n, span in enumerate(spans)
    ]
    for copy in copies:
        copy.start()
    for n in range(far.shape[0] // CAP):
        kind, chip = far_block(place, n)
        pair = hidden[pair_rows(chip), :].astype(F32)
        far[n * CAP : (n + 1) * CAP, :] = jnp.where(kind == 0, pair[:CAP], pair[CAP:])
    for n, at in enumerate(starts):
        copies[n].wait()
        to = min(at + TILE, units)
        left = far[:, at:to].astype(BF16)
        for col in range(0, width, 512):
            span = slice(col, col + 512)
            turned[span, at:to] = held[at:to, span].T
            value = jnp.dot(left, held[at:to, span], preferred_element_type=F32)
            ahead[:, span] = value if n == 0 else ahead[:, span] + value


def turn(place, hidden, weight):
    units, width = weight.shape
    height = hidden.shape[0] // 4
    return pl.pallas_call(
        turn_kernel,
        out_shape=(pltpu.VMEM((width, units), BF16), pltpu.VMEM((height, width), F32)),
        in_specs=[smem(), vmem(), anywhere()],
        out_specs=(vmem(), vmem()),
        scratch_shapes=[
            pltpu.VMEM((units, width), BF16),
            pltpu.VMEM((height, units), F32),
            pltpu.SemaphoreType.DMA((pl.cdiv(units, TILE),)),
        ],
        compiler_params=params(),
        cost_estimate=small(),
    )(place, hidden, pltpu.with_memory_space_constraint(weight, pltpu.HBM))


def near_kernel(place, mine, theirs, turned, out, gates, packed):
    pack(place[3], (mine, theirs), packed, gates)
    multiply(packed, turned, out)


def near_of(place, mine, theirs, turned):
    width, units = turned.shape
    height = 2 * mine.shape[0] // ROWS * CAP
    return pl.pallas_call(
        near_kernel,
        out_shape=(pltpu.VMEM((height, units), F32), pltpu.VMEM((height, META), F32)),
        in_specs=[smem()] + [vmem()] * 3,
        out_specs=(vmem(), vmem()),
        scratch_shapes=[pltpu.VMEM((height, width), BF16)],
        compiler_params=params(),
        cost_estimate=small(),
    )(place, mine, theirs, turned)


def chip_of(place, i, j):
    return ((place[0] + (i + 4)) % 4) * 4 + (place[1] + (j + 4)) % 4


def pair_rows(chip):
    return pl.ds(pl.multiple_of(chip * (2 * CAP), 16), 2 * CAP)


def block_rows(place, kind, group, along):
    which = jnp.where(place[2] == kind, 0, 1)
    return pl.ds(pl.multiple_of((which * group + along) * CAP, 8), CAP)


def finish(chip, pieces, saved, sums, write):
    diagonal = lax.broadcasted_iota(jnp.int32, (CAP, META), 0) == lax.broadcasted_iota(
        jnp.int32, (CAP, META), 1
    )
    scales = [None if p is None or p[1] is None else p[1][p[2], :] for p in pieces]
    totals = [jnp.zeros((CAP, META), F32) for _ in pieces]
    for col in range(0, saved.shape[1], META):
        span = slice(col, col + META)
        factor = saved[pair_rows(chip), span].astype(F32)
        scaled = []
        for kind, piece in enumerate(pieces):
            if piece is None:
                scaled.append(None)
                continue
            value = piece[0][piece[2], span]
            if scales[kind] is not None:
                totals[kind] += factor[kind * CAP : (kind + 1) * CAP] * value
                value = scales[kind] * value
            scaled.append(value)
        write(span, scaled)
    for kind, scale in enumerate(scales):
        if scale is not None:
            total = jnp.sum(totals[kind], axis=1, keepdims=True)
            sums[pl.ds(chip * 2 + kind, 1), :] = jnp.sum(
                jnp.where(diagonal, total, 0.0), axis=0, keepdims=True
            )


def staged(stage, slot):
    def write(span, scaled):
        stage[slot, :, span] = jnp.concatenate(scaled, axis=0).astype(BF16)

    return write


def mid_kernel(
    place, low, high, low_other, high_other, turned, hidden, near, near_gates,
    grad, sums, halves, packed, mid, mid_gates, stage, sems,
):
    pack(place[3], (low, high, low_other, high_other), packed, mid_gates)
    multiply(packed, turned, mid)

    def piece(kind, along, across):
        a = OFFSETS.index(along)
        if across == 0:
            return near, near_gates, block_rows(place, kind, 4, a)
        return mid, mid_gates, block_rows(place, kind, 8, (0 if across == -1 else 4) + a)

    copies = []
    for i in (0, -1, 1):
        for j in (0, -1, 1):
            chip, slot = chip_of(place, i, j), len(copies)
            finish(chip, (piece(0, i, j), piece(1, j, i)), hidden, sums, staged(stage, slot))
            copy = pltpu.make_async_copy(stage.at[slot], grad.at[pair_rows(chip), :], sems.at[slot])
            copy.start()
            copies.append(copy)
    for n, (kind, i, j) in enumerate(HALVES):
        def write(span, scaled, kind=kind, n=n):
            halves[n * CAP : (n + 1) * CAP, span] = scaled[kind]

        pieces = (piece(0, i, j), None) if kind == 0 else (None, piece(1, j, i))
        finish(chip_of(place, i, j), pieces, hidden, sums, write)
    for copy in copies:
        copy.wait()


def mid_of(place, tokens, turned, hidden, near, near_gates):
    width, units = turned.shape
    height = sum(t.shape[0] for t in tokens) // ROWS * CAP
    return pl.pallas_call(
        mid_kernel,
        out_shape=(
            jax.ShapeDtypeStruct(hidden.shape, BF16),
            pltpu.VMEM((hidden.shape[0] // CAP, META), F32),
            pltpu.VMEM((len(HALVES) * CAP, units), F32),
        ),
        in_specs=[smem()] + [vmem()] * 8,
        out_specs=(anywhere(), vmem(), vmem()),
        scratch_shapes=[
            pltpu.VMEM((height, width), BF16),
            pltpu.VMEM((height, units), F32),
            pltpu.VMEM((height, META), F32),
            pltpu.VMEM((9, 2 * CAP, units), BF16),
            pltpu.SemaphoreType.DMA((9,)),
        ],
        compiler_params=params(),
        cost_estimate=small(),
    )(place, *tokens, turned, hidden, near, near_gates)


def sums_kernel(place, mine, theirs, ahead, early, sums, packed, gates):
    sums[...] = early[...]
    pack(place[3], (mine, theirs), packed, gates)
    height, width = packed.shape
    diagonal = lax.broadcasted_iota(jnp.int32, (CAP, META), 0) == lax.broadcasted_iota(
        jnp.int32, (CAP, META), 1
    )
    for n in range(height // CAP):
        block = slice(n * CAP, (n + 1) * CAP)
        total = jnp.zeros((CAP, META), F32)
        for col in range(0, width, META):
            span = slice(col, col + META)
            total += packed[block, span].astype(F32) * ahead[block, span]
        total = jnp.sum(total, axis=1, keepdims=True)
        kind, chip = far_block(place, n)
        sums[pl.ds(chip * 2 + kind, 1), :] = jnp.sum(
            jnp.where(diagonal, total, 0.0), axis=0, keepdims=True
        )


def sums_of(place, mine, theirs, ahead, early):
    height, width = ahead.shape
    return pl.pallas_call(
        sums_kernel,
        out_shape=(
            pltpu.VMEM(early.shape, F32),
            pltpu.VMEM((height, width), BF16),
            pltpu.VMEM((height, META), F32),
        ),
        in_specs=[smem()] + [vmem()] * 4,
        out_specs=(vmem(), vmem(), vmem()),
        compiler_params=params(),
        cost_estimate=small(),
    )(place, mine, theirs, ahead, early)


def far_kernel(place, packed, gates, turned, halves, _, grad, held, far, stage, sems, loads):
    units = far.shape[1]
    spans = [pl.ds(at, 512) for at in range(0, held.shape[0], 512)]
    copies = [
        pltpu.make_async_copy(turned.at[span, :], held.at[span, :], loads.at[n])
        for n, span in enumerate(spans)
    ]
    for copy in copies:
        copy.start()
    for n, span in enumerate(spans):
        copies[n].wait()
        at = slice(span.start, span.start + span.size)
        value = jnp.dot(packed[:, at], held[at, :], preferred_element_type=F32)
        far[...] = value if n == 0 else far[...] + value
    copies = []
    for i in OFFSETS:
        for j in OFFSETS:
            if i != 2 and j != 2:
                continue
            pieces = []
            for kind, along, across in ((0, i, j), (1, j, i)):
                if across == 2:
                    span = block_rows(place, kind, 4, OFFSETS.index(along))
                    pieces.append((far, gates[span, :], span))
                else:
                    n = HALVES.index((kind, i, j))
                    pieces.append((halves, None, pl.ds(n * CAP, CAP)))
            chip, slot = chip_of(place, i, j), len(copies)
            for col in range(0, units, META):
                span = slice(col, col + META)
                scaled = [
                    ref[at, span] if scale is None else scale * ref[at, span]
                    for ref, scale, at in pieces
                ]
                stage[slot, :, span] = jnp.concatenate(scaled, axis=0).astype(BF16)
            copy = pltpu.make_async_copy(stage.at[slot], grad.at[pair_rows(chip), :], sems.at[slot])
            copy.start()
            copies.append(copy)
    for copy in copies:
        copy.wait()


def far_of(place, packed, gates, turned, halves, grad):
    width, units = turned.shape
    height = packed.shape[0]
    return pl.pallas_call(
        far_kernel,
        out_shape=jax.ShapeDtypeStruct(grad.shape, BF16),
        in_specs=[smem(), vmem(), vmem(), anywhere(), vmem(), anywhere()],
        out_specs=anywhere(),
        scratch_shapes=[
            pltpu.VMEM((width, units), BF16),
            pltpu.VMEM((height, units), F32),
            pltpu.VMEM((7, 2 * CAP, units), BF16),
            pltpu.SemaphoreType.DMA((7,)),
            pltpu.SemaphoreType.DMA((width // 512,)),
        ],
        input_output_aliases={5: 0},
        compiler_params=params(),
        cost_estimate=pl.CostEstimate(
            flops=2 * height * units * turned.shape[0], bytes_accessed=1, transcendentals=0
        ),
    )(place, packed, gates, pltpu.with_memory_space_constraint(turned, pltpu.HBM), halves, grad)


def gather_kernel(totals, lines, out):
    quarter = totals.shape[0] // 4
    total = totals[0:quarter, :]
    for n in range(1, 4):
        total = total + totals[n * quarter : (n + 1) * quarter, :]
    pick = (lax.broadcasted_iota(jnp.int32, (META, META), 0) == lines[0:1, :]).astype(F32)
    line = jnp.dot(total, pick, precision=lax.Precision.HIGHEST, preferred_element_type=F32)
    chosen = lax.broadcasted_iota(jnp.int32, line.shape, 0) == lines[1:2, :]
    line = jnp.sum(jnp.where(chosen, line, 0.0), axis=0, keepdims=True)
    tokens = out.shape[1]
    for k in range(TOP):
        out[k : k + 1, :] = line[:, k * tokens : (k + 1) * tokens]


def on_device(handoff, expert_ids, gates, down_weight, hidden):
    dp, expert = lax.axis_index("dp"), lax.axis_index("expert")
    place = jnp.stack([dp, expert // 2, expert % 2, expert]).astype(jnp.int32)
    ids = expert_ids[0].T
    weight, saved = down_weight[0, 0], hidden[0, 0]
    incoming = moved(handoff[0], previous_section)
    meta, lines, place = meta_of(place, ids, gates[0].T)
    incoming, meta, lines, place = lax.optimization_barrier((incoming, meta, lines, place))
    own = jnp.concatenate([incoming, meta], axis=1)
    own, place = lax.optimization_barrier((own, place))

    ahead, back, across = [moved(own, first(k)) for k in (1, 3, 2)]
    turned, ahead_far = turn(place, saved, weight)
    ahead, back, across, turned, ahead_far = lax.optimization_barrier(
        (ahead, back, across, turned, ahead_far)
    )
    near = rows(own, ahead, back, across)
    low, high = moved(near, second(1)), moved(near, second(3))
    near_other = moved(near, other_core)
    near_done = near_of(place, near, near_other, turned)
    low, high, *near_done = lax.optimization_barrier((low, high, *near_done))
    left, right = halves_of(high, low)
    far = moved(left, second(3)), moved(right, second(1))
    tokens = low, high, moved(low, other_core), moved(high, other_core)
    grad, sums, halves = mid_of(place, tokens, turned, saved, *near_done)
    *far, grad, sums, halves = lax.optimization_barrier((*far, grad, sums, halves))
    far = join(*far)
    far_other = moved(far, other_core)
    sums, packed, far_gates = sums_of(place, far, far_other, ahead_far, sums)
    totals = lax.all_to_all(sums, ("dp", "expert"), split_axis=0, concat_axis=0, tiled=True)
    grad = far_of(place, packed, far_gates, turned, halves, grad)
    gate_grad = pl.pallas_call(
        gather_kernel,
        out_shape=jax.ShapeDtypeStruct(ids.shape, F32),
        in_specs=[vmem()] * 2,
        out_specs=vmem(),
        compiler_params=params(2),
    )(totals, lines)
    return (grad[None, None], gate_grad.T[None])


def solution(mesh):
    return jax.shard_map(
        on_device,
        mesh=mesh,
        in_specs=(
            P("pipe", ("dp", "expert"), None),
            P("pipe", ("dp", "expert"), None),
            P("pipe", ("dp", "expert"), None),
            P("pipe", "expert", "dp", None),
            P("pipe", "expert", None, "dp"),
        ),
        out_specs=(P("pipe", "expert", None, "dp"), P("pipe", ("dp", "expert"), None)),
        check_vma=False,
    )
```

```python
import functools

import jax
import jax.numpy as jnp
from jax import lax
from jax.experimental import pallas as pl
from jax.experimental.pallas import tpu as pltpu
from jax.sharding import PartitionSpec as P

EXPERTS = 8
TOP = 4
CAP = 24
ROWS = 32
META = 128
TILE = 256
OFFSETS = (0, -1, 1, 2)
HALVES = tuple((0, 2, j) for j in (0, -1, 1)) + tuple((1, i, 2) for i in (0, -1, 1))
AXES = ("pipe", "dp", "expert")
VMEM_LIMIT = 20
F32 = jnp.float32
BF16 = jnp.bfloat16


def moved(x, to):
    nz, nx, ne = (lax.axis_size(a) for a in AXES)
    ny = ne // 2

    def index(z, i, j, c):
        return ((z % nz) * nx + i % nx) * ne + (j % ny) * 2 + c

    pairs = [
        (index(z, i, j, c), index(*to(z, i, j, c)))
        for z in range(nz)
        for i in range(nx)
        for j in range(ny)
        for c in range(2)
    ]
    return lax.ppermute(x, AXES, pairs)


def first(k):
    return lambda z, i, j, c: (z, i + k, j, c) if c == 0 else (z, i, j + k, c)


def second(k):
    return lambda z, i, j, c: (z, i, j + k, c) if c == 0 else (z, i + k, j, c)


def other_core(z, i, j, c):
    return (z, i, j, 1 - c)


def previous_section(z, i, j, c):
    return (z - 1, i, j, c)


def rows(*parts):
    return jnp.concatenate(parts, axis=0)


def pack(expert, token_refs, packed, gates, weights=None):
    dots = []
    lane = lax.broadcasted_iota(jnp.int32, (16, META), 1)
    line = lax.broadcasted_iota(jnp.int32, (16, META), 0)
    pick = ((line == 0) & (lane == expert)).astype(F32).astype(BF16)
    spread = (
        lax.broadcasted_iota(jnp.int32, (META, META), 0) == EXPERTS + expert
    ).astype(F32).astype(BF16)
    at = 0
    for ref in token_refs:
        count, width = ref.shape
        width = width - META
        height = count // ROWS * CAP
        meta = ref[:, width:]
        slot = lax.dot_general(pick, meta, (((1,), (1,)), ((), ())), preferred_element_type=F32)[0:1, :]
        block = lax.broadcasted_iota(jnp.int32, (1, count), 1) // ROWS
        target = jnp.where(slot >= 0.0, slot.astype(jnp.int32) + block * CAP, -1)
        chosen = (
            lax.broadcasted_iota(jnp.int32, (height, count), 0) == target
        ).astype(F32).astype(BF16)
        dot = jnp.zeros((height, META), F32)
        for start in range(0, width, 512):
            value = jnp.dot(chosen, ref[:, start : start + 512], preferred_element_type=F32)
            packed[at : at + height, start : start + 512] = value.astype(BF16)
            if weights is None:
                continue
            for col in range(0, 512, META):
                factor = weights[at : at + height, start + col : start + col + META]
                dot += value[:, col : col + META] * factor
        dots.append(jnp.sum(dot, axis=1, keepdims=True))
        own = jnp.dot(chosen, meta, preferred_element_type=F32).astype(BF16)
        gates[at : at + height, :] = jnp.dot(own, spread, preferred_element_type=F32)
        at += height
    return dots


def multiply(packed, turned, out):
    units = turned.shape[1]
    for at in range(0, units, TILE):
        size = min(TILE, units - at)
        out[:, at : at + size] = jnp.dot(
            packed[...], turned[:, at : at + size], preferred_element_type=F32
        )


def smem():
    return pl.BlockSpec(memory_space=pltpu.SMEM)


def vmem():
    return pl.BlockSpec(memory_space=pltpu.VMEM)


def anywhere():
    return pl.BlockSpec(memory_space=pl.ANY)


def params(mebibytes=VMEM_LIMIT):
    return pltpu.CompilerParams(vmem_limit_bytes=mebibytes << 20)


def small():
    return pl.CostEstimate(flops=1, bytes_accessed=1, transcendentals=0)


def meta_kernel(place, ids, gates, meta, lines, spot):
    for n in range(4):
        spot[n] = place[n]
    tokens = ids.shape[1]
    expert = lax.broadcasted_iota(jnp.int32, (EXPERTS, tokens), 0)
    named = [ids[k : k + 1, :] == expert for k in range(TOP)]
    some = jnp.zeros((EXPERTS, tokens), F32)
    gate = jnp.zeros((EXPERTS, tokens), F32)
    weights = gates[...].astype(F32)
    for k in range(TOP):
        some = jnp.where(named[k], 1.0, some)
        gate = jnp.where(named[k], weights[k : k + 1, :], gate)
    row = lax.broadcasted_iota(jnp.int32, (tokens, tokens), 0)
    col = lax.broadcasted_iota(jnp.int32, (tokens, tokens), 1)
    earlier = (row < col).astype(F32).astype(BF16)
    before = jnp.dot(some.astype(BF16), earlier, preferred_element_type=F32)
    slot = jnp.where(some > 0.0, before, -1.0)
    lines[...] = jnp.zeros(lines.shape, jnp.int32)
    for k in range(TOP):
        own = jnp.sum(jnp.where(named[k], before, 0.0), axis=0, keepdims=True)
        lines[0:1, k * tokens : (k + 1) * tokens] = own.astype(jnp.int32)
        lines[1:2, k * tokens : (k + 1) * tokens] = ids[k : k + 1, :]
    table = jnp.concatenate(
        [slot, gate, jnp.zeros((META - 2 * EXPERTS, tokens), F32)], axis=0
    ).astype(BF16)
    unit = (row == col).astype(F32).astype(BF16)
    meta[...] = lax.dot_general(
        unit, table, (((1,), (1,)), ((), ())), preferred_element_type=F32
    ).astype(BF16)


def meta_of(place, ids, gates):
    return pl.pallas_call(
        meta_kernel,
        out_shape=(
            jax.ShapeDtypeStruct((ids.shape[1], META), BF16),
            jax.ShapeDtypeStruct((8, META), jnp.int32),
            jax.ShapeDtypeStruct((4,), jnp.int32),
        ),
        in_specs=[smem(), vmem(), vmem()],
        out_specs=(vmem(), vmem(), smem()),
        compiler_params=params(2),
    )(place, ids, gates)


def join_kernel(*refs):
    at = 0
    for ref in refs[:-1]:
        refs[-1][at : at + ref.shape[0], :] = ref[...]
        at += ref.shape[0]


def join(*parts):
    shape = (sum(p.shape[0] for p in parts), parts[0].shape[1])
    return pl.pallas_call(
        join_kernel,
        out_shape=pltpu.VMEM(shape, parts[0].dtype),
        in_specs=[vmem()] * len(parts),
        out_specs=vmem(),
        compiler_params=params(6),
        cost_estimate=small(),
    )(*parts)


def halves_kernel(high, low, first_half, second_half):
    half = first_half.shape[0]
    first_half[...] = high[:half, :]
    second_half[...] = low[half:, :]


def halves_of(high, low):
    shape = (high.shape[0] // 2, high.shape[1])
    return pl.pallas_call(
        halves_kernel,
        out_shape=(pltpu.VMEM(shape, BF16), pltpu.VMEM(shape, BF16)),
        in_specs=[vmem()] * 2,
        out_specs=(vmem(), vmem()),
        compiler_params=params(6),
        cost_estimate=small(),
    )(high, low)


def far_block(place, n):
    which, a = divmod(n, 4)
    kind = place[2] if which == 0 else 1 - place[2]
    x = jnp.where(kind == 0, OFFSETS[a], 2)
    y = jnp.where(kind == 0, 2, OFFSETS[a])
    return kind, chip_of(place, x, y)


def turn_kernel(place, weight, turned, held, sems):
    units, width = weight.shape
    copies = [
        pltpu.make_async_copy(
            weight.at[pl.ds(at, META), :], held.at[pl.ds(at, META), :], sems.at[at // META]
        )
        for at in range(0, units, META)
    ]
    for copy in copies:
        copy.start()
    for copy, at in zip(copies, range(0, units, META)):
        copy.wait()
        for col in range(0, width, 512):
            turned[col : col + 512, at : at + META] = held[at : at + META, col : col + 512].T


def turn(place, weight):
    units, width = weight.shape
    return pl.pallas_call(
        turn_kernel,
        out_shape=pltpu.VMEM((width, units), BF16),
        in_specs=[smem(), anywhere()],
        out_specs=vmem(),
        scratch_shapes=[
            pltpu.VMEM((units, width), BF16),
            pltpu.SemaphoreType.DMA((units // META,)),
        ],
        compiler_params=params(),
        cost_estimate=small(),
    )(place, pltpu.with_memory_space_constraint(weight, pltpu.HBM))


def ahead_kernel(place, hidden, weight, out, held, far, sems):
    units, width = weight.shape
    spans = [pl.ds(at, min(512, units - at)) for at in range(0, units, 512)]
    copies = [
        pltpu.make_async_copy(weight.at[span, :], held.at[span, :], sems.at[n])
        for n, span in enumerate(spans)
    ]
    for copy in copies:
        copy.start()
    for n in range(far.shape[0] // CAP):
        kind, chip = far_block(place, n)
        pair = hidden[pair_rows(chip), :].astype(F32)
        far[n * CAP : (n + 1) * CAP, :] = jnp.where(kind == 0, pair[:CAP], pair[CAP:])
    for n, span in enumerate(spans):
        copies[n].wait()
        at = slice(span.start, span.start + span.size)
        left = far[:, at].astype(BF16)
        for col in range(0, width, 512):
            value = jnp.dot(left, held[at, col : col + 512], preferred_element_type=F32)
            if n:
                value = out[:, col : col + 512] + value
            out[:, col : col + 512] = value


def ahead_of(place, hidden, weight):
    units, width = weight.shape
    height = hidden.shape[0] // 4
    return pl.pallas_call(
        ahead_kernel,
        out_shape=pltpu.VMEM((height, width), F32),
        in_specs=[smem(), vmem(), anywhere()],
        out_specs=vmem(),
        scratch_shapes=[
            pltpu.VMEM((units, width), BF16),
            pltpu.VMEM((height, units), F32),
            pltpu.SemaphoreType.DMA((pl.cdiv(units, 512),)),
        ],
        compiler_params=params(),
        cost_estimate=small(),
    )(place, hidden, pltpu.with_memory_space_constraint(weight, pltpu.HBM))


def near_kernel(place, mine, theirs, turned, out, gates, packed):
    pack(place[3], (mine, theirs), packed, gates)
    multiply(packed, turned, out)


def near_of(place, mine, theirs, turned):
    width, units = turned.shape
    height = 2 * mine.shape[0] // ROWS * CAP
    return pl.pallas_call(
        near_kernel,
        out_shape=(pltpu.VMEM((height, units), F32), pltpu.VMEM((height, META), F32)),
        in_specs=[smem()] + [vmem()] * 3,
        out_specs=(vmem(), vmem()),
        scratch_shapes=[pltpu.VMEM((height, width), BF16)],
        compiler_params=params(),
        cost_estimate=small(),
    )(place, mine, theirs, turned)


def chip_of(place, i, j):
    return ((place[0] + (i + 4)) % 4) * 4 + (place[1] + (j + 4)) % 4


def pair_rows(chip):
    return pl.ds(pl.multiple_of(chip * (2 * CAP), 16), 2 * CAP)


def block_rows(place, kind, group, along):
    which = jnp.where(place[2] == kind, 0, 1)
    return pl.ds(pl.multiple_of((which * group + along) * CAP, 8), CAP)


def finish(chip, pieces, saved, sums, write):
    diagonal = lax.broadcasted_iota(jnp.int32, (CAP, META), 0) == lax.broadcasted_iota(
        jnp.int32, (CAP, META), 1
    )
    scales = [None if p is None or p[1] is None else p[1][p[2], :] for p in pieces]
    totals = [jnp.zeros((CAP, META), F32) for _ in pieces]
    for col in range(0, saved.shape[1], META):
        span = slice(col, col + META)
        factor = saved[pair_rows(chip), span].astype(F32)
        scaled = []
        for kind, piece in enumerate(pieces):
            if piece is None:
                scaled.append(None)
                continue
            value = piece[0][piece[2], span]
            if scales[kind] is not None:
                totals[kind] += factor[kind * CAP : (kind + 1) * CAP] * value
                value = scales[kind] * value
            scaled.append(value)
        write(span, scaled)
    for kind, scale in enumerate(scales):
        if scale is not None:
            total = jnp.sum(totals[kind], axis=1, keepdims=True)
            sums[pl.ds(chip * 2 + kind, 1), :] = jnp.sum(
                jnp.where(diagonal, total, 0.0), axis=0, keepdims=True
            )


def staged(stage, slot):
    def write(span, scaled):
        stage[slot, :, span] = jnp.concatenate(scaled, axis=0).astype(BF16)

    return write


def mid_kernel(
    place, low, high, low_other, high_other, turned, hidden, near, near_gates,
    grad, sums, halves, packed, mid, mid_gates, stage, sems,
):
    pack(place[3], (low, high, low_other, high_other), packed, mid_gates)
    multiply(packed, turned, mid)

    def piece(kind, along, across):
        a = OFFSETS.index(along)
        if across == 0:
            return near, near_gates, block_rows(place, kind, 4, a)
        return mid, mid_gates, block_rows(place, kind, 8, (0 if across == -1 else 4) + a)

    copies = []
    for i in (0, -1, 1):
        for j in (0, -1, 1):
            chip, slot = chip_of(place, i, j), len(copies)
            finish(chip, (piece(0, i, j), piece(1, j, i)), hidden, sums, staged(stage, slot))
            copy = pltpu.make_async_copy(stage.at[slot], grad.at[pair_rows(chip), :], sems.at[slot])
            copy.start()
            copies.append(copy)
    for n, (kind, i, j) in enumerate(HALVES):
        def write(span, scaled, kind=kind, n=n):
            halves[n * CAP : (n + 1) * CAP, span] = scaled[kind]

        pieces = (piece(0, i, j), None) if kind == 0 else (None, piece(1, j, i))
        finish(chip_of(place, i, j), pieces, hidden, sums, write)
    for copy in copies:
        copy.wait()


def mid_of(place, tokens, turned, hidden, near, near_gates):
    width, units = turned.shape
    height = sum(t.shape[0] for t in tokens) // ROWS * CAP
    return pl.pallas_call(
        mid_kernel,
        out_shape=(
            jax.ShapeDtypeStruct(hidden.shape, BF16),
            pltpu.VMEM((hidden.shape[0] // CAP, META), F32),
            pltpu.VMEM((len(HALVES) * CAP, units), F32),
        ),
        in_specs=[smem()] + [vmem()] * 8,
        out_specs=(anywhere(), vmem(), vmem()),
        scratch_shapes=[
            pltpu.VMEM((height, width), BF16),
            pltpu.VMEM((height, units), F32),
            pltpu.VMEM((height, META), F32),
            pltpu.VMEM((9, 2 * CAP, units), BF16),
            pltpu.SemaphoreType.DMA((9,)),
        ],
        compiler_params=params(),
        cost_estimate=small(),
    )(place, *tokens, turned, hidden, near, near_gates)


def sums_kernel(which, place, tokens, ahead, early, sums, packed, gates):
    sums[...] = early[...]
    height = packed.shape[0]
    at = slice(which * height, (which + 1) * height)
    (total,) = pack(place[3], (tokens,), packed, gates, ahead.at[at, :])
    diagonal = lax.broadcasted_iota(jnp.int32, (CAP, META), 0) == lax.broadcasted_iota(
        jnp.int32, (CAP, META), 1
    )
    for n in range(4):
        kind, chip = far_block(place, which * 4 + n)
        line = jnp.where(diagonal, total[n * CAP : (n + 1) * CAP], 0.0)
        sums[pl.ds(chip * 2 + kind, 1), :] = jnp.sum(line, axis=0, keepdims=True)


def sums_of(which, place, tokens, ahead, early):
    height, width = ahead.shape
    return pl.pallas_call(
        functools.partial(sums_kernel, which),
        out_shape=(
            pltpu.VMEM(early.shape, F32),
            pltpu.VMEM((height // 2, width), BF16),
            pltpu.VMEM((height // 2, META), F32),
        ),
        in_specs=[smem()] + [vmem()] * 3,
        out_specs=(vmem(), vmem(), vmem()),
        compiler_params=params(),
        cost_estimate=small(),
    )(place, tokens, ahead, early)


def far_kernel(
    place, mine, theirs, gates, other_gates, turned, halves, _, grad, held, far, far_scales, stage, sems, loads
):
    units = far.shape[1]
    spans = [pl.ds(at, 512) for at in range(0, held.shape[0], 512)]
    copies = [
        pltpu.make_async_copy(turned.at[span, :], held.at[span, :], loads.at[n])
        for n, span in enumerate(spans)
    ]
    for copy in copies:
        copy.start()
    for n, span in enumerate(spans):
        copies[n].wait()
        at = slice(span.start, span.start + span.size)
        rows_of = jnp.concatenate([mine[:, at], theirs[:, at]], axis=0)
        value = jnp.dot(rows_of, held[at, :], preferred_element_type=F32)
        far[...] = value if n == 0 else far[...] + value
    copies = []
    scales = jnp.concatenate([gates[...], other_gates[...]], axis=0)
    far_scales[...] = scales
    for i in OFFSETS:
        for j in OFFSETS:
            if i != 2 and j != 2:
                continue
            pieces = []
            for kind, along, across in ((0, i, j), (1, j, i)):
                if across == 2:
                    span = block_rows(place, kind, 4, OFFSETS.index(along))
                    pieces.append((far, far_scales[span, :], span))
                else:
                    n = HALVES.index((kind, i, j))
                    pieces.append((halves, None, pl.ds(n * CAP, CAP)))
            chip, slot = chip_of(place, i, j), len(copies)
            for col in range(0, units, META):
                span = slice(col, col + META)
                scaled = [
                    ref[at, span] if scale is None else scale * ref[at, span]
                    for ref, scale, at in pieces
                ]
                stage[slot, :, span] = jnp.concatenate(scaled, axis=0).astype(BF16)
            copy = pltpu.make_async_copy(stage.at[slot], grad.at[pair_rows(chip), :], sems.at[slot])
            copy.start()
            copies.append(copy)
    for copy in copies:
        copy.wait()


def far_of(place, mine, theirs, gates, other_gates, turned, halves, grad):
    width, units = turned.shape
    height = 2 * mine.shape[0]
    return pl.pallas_call(
        far_kernel,
        out_shape=jax.ShapeDtypeStruct(grad.shape, BF16),
        in_specs=[smem()] + [vmem()] * 4 + [anywhere(), vmem(), anywhere()],
        out_specs=anywhere(),
        scratch_shapes=[
            pltpu.VMEM((width, units), BF16),
            pltpu.VMEM((height, units), F32),
            pltpu.VMEM((height, META), F32),
            pltpu.VMEM((7, 2 * CAP, units), BF16),
            pltpu.SemaphoreType.DMA((7,)),
            pltpu.SemaphoreType.DMA((width // 512,)),
        ],
        input_output_aliases={7: 0},
        compiler_params=params(),
        cost_estimate=pl.CostEstimate(
            flops=2 * height * units * turned.shape[0], bytes_accessed=1, transcendentals=0
        ),
    )(
        place, mine, theirs, gates, other_gates,
        pltpu.with_memory_space_constraint(turned, pltpu.HBM), halves, grad,
    )


def gather_kernel(totals, lines, out):
    quarter = totals.shape[0] // 4
    total = totals[0:quarter, :]
    for n in range(1, 4):
        total = total + totals[n * quarter : (n + 1) * quarter, :]
    pick = (lax.broadcasted_iota(jnp.int32, (META, META), 0) == lines[0:1, :]).astype(F32)
    line = jnp.dot(total, pick, precision=lax.Precision.HIGHEST, preferred_element_type=F32)
    chosen = lax.broadcasted_iota(jnp.int32, line.shape, 0) == lines[1:2, :]
    line = jnp.sum(jnp.where(chosen, line, 0.0), axis=0, keepdims=True)
    tokens = out.shape[1]
    for k in range(TOP):
        out[k : k + 1, :] = line[:, k * tokens : (k + 1) * tokens]


def on_device(handoff, expert_ids, gates, down_weight, hidden):
    dp, expert = lax.axis_index("dp"), lax.axis_index("expert")
    place = jnp.stack([dp, expert // 2, expert % 2, expert]).astype(jnp.int32)
    ids = expert_ids[0].T
    weight, saved = down_weight[0, 0], hidden[0, 0]
    incoming = moved(handoff[0], previous_section)
    meta, lines, place = meta_of(place, ids, gates[0].T)
    incoming, meta, lines, place = lax.optimization_barrier((incoming, meta, lines, place))
    own = jnp.concatenate([incoming, meta], axis=1)
    own, place = lax.optimization_barrier((own, place))

    ahead, back, across = [moved(own, first(k)) for k in (1, 3, 2)]
    turned = turn(place, weight)
    ahead, back, across, turned = lax.optimization_barrier((ahead, back, across, turned))
    near = rows(own, ahead, back, across)
    low, high = moved(near, second(1)), moved(near, second(3))
    near_other = moved(near, other_core)
    near_other, later = lax.optimization_barrier((near_other, place))
    near_done = near_of(place, near, near_other, turned)
    ahead_far = ahead_of(later, saved, weight)
    low, high, ahead_far, *near_done = lax.optimization_barrier((low, high, ahead_far, *near_done))
    left, right = halves_of(high, low)
    far = moved(left, second(3)), moved(right, second(1))
    tokens = low, high, moved(low, other_core), moved(high, other_core)
    grad, sums, halves = mid_of(place, tokens, turned, saved, *near_done)
    *far, grad, sums, halves = lax.optimization_barrier((*far, grad, sums, halves))
    far = join(*far)
    far_other = moved(far, other_core)
    sums, mine, far_gates = sums_of(0, place, far, ahead_far, sums)
    sums, theirs, other_gates = sums_of(1, place, far_other, ahead_far, sums)
    totals = lax.all_to_all(sums, ("dp", "expert"), split_axis=0, concat_axis=0, tiled=True)
    grad = far_of(place, mine, theirs, far_gates, other_gates, turned, halves, grad)
    gate_grad = pl.pallas_call(
        gather_kernel,
        out_shape=jax.ShapeDtypeStruct(ids.shape, F32),
        in_specs=[vmem()] * 2,
        out_specs=vmem(),
        compiler_params=params(2),
    )(totals, lines)
    return (grad[None, None], gate_grad.T[None])


def solution(mesh):
    return jax.shard_map(
        on_device,
        mesh=mesh,
        in_specs=(
            P("pipe", ("dp", "expert"), None),
            P("pipe", ("dp", "expert"), None),
            P("pipe", ("dp", "expert"), None),
            P("pipe", "expert", "dp", None),
            P("pipe", "expert", None, "dp"),
        ),
        out_specs=(P("pipe", "expert", None, "dp"), P("pipe", ("dp", "expert"), None)),
        check_vma=False,
    )
```

```python
import jax
import jax.numpy as jnp
from jax import lax
from jax.experimental import pallas as pl
from jax.experimental.pallas import tpu as pltpu
from jax.sharding import PartitionSpec as P

EXPERTS = 8
TOP = 4
CAP = 24
ROWS = 32
META = 128
LANES = 32
TILE = 256
OFFSETS = (0, -1, 1, 2)
HALVES = tuple((0, 2, j) for j in (0, -1, 1)) + tuple((1, i, 2) for i in (0, -1, 1))
AXES = ("pipe", "dp", "expert")
VMEM_LIMIT = 20
F32 = jnp.float32
BF16 = jnp.bfloat16


def moved(x, to):
    nz, nx, ne = (lax.axis_size(a) for a in AXES)
    ny = ne // 2

    def index(z, i, j, c):
        return ((z % nz) * nx + i % nx) * ne + (j % ny) * 2 + c

    pairs = [
        (index(z, i, j, c), index(*to(z, i, j, c)))
        for z in range(nz)
        for i in range(nx)
        for j in range(ny)
        for c in range(2)
    ]
    return lax.ppermute(x, AXES, pairs)


def first(k):
    return lambda z, i, j, c: (z, i + k, j, c) if c == 0 else (z, i, j + k, c)


def second(k):
    return lambda z, i, j, c: (z, i, j + k, c) if c == 0 else (z, i + k, j, c)


def other_core(z, i, j, c):
    return (z, i, j, 1 - c)


def previous_section(z, i, j, c):
    return (z - 1, i, j, c)


def rows(*parts):
    return jnp.concatenate(parts, axis=0)


def pack(expert, token_refs, packed, gates, weights=None):
    dots = []
    lane = lax.broadcasted_iota(jnp.int32, (16, META), 1)
    line = lax.broadcasted_iota(jnp.int32, (16, META), 0)
    pick = ((line == 0) & (lane == expert)).astype(F32).astype(BF16)
    spread = (
        lax.broadcasted_iota(jnp.int32, (META, META), 0) == EXPERTS + expert
    ).astype(F32).astype(BF16)
    at = 0
    for ref in token_refs:
        count, width = ref.shape
        width = width - META
        height = count // ROWS * CAP
        meta = ref[:, width:]
        slot = lax.dot_general(pick, meta, (((1,), (1,)), ((), ())), preferred_element_type=F32)[0:1, :]
        block = lax.broadcasted_iota(jnp.int32, (1, count), 1) // ROWS
        target = jnp.where(slot >= 0.0, slot.astype(jnp.int32) + block * CAP, -1)
        chosen = (
            lax.broadcasted_iota(jnp.int32, (height, count), 0) == target
        ).astype(F32).astype(BF16)
        dot = jnp.zeros((height, META), F32)
        for start in range(0, width, 512):
            value = jnp.dot(chosen, ref[:, start : start + 512], preferred_element_type=F32)
            if packed is not None:
                packed[at : at + height, start : start + 512] = value.astype(BF16)
            if weights is None:
                continue
            for col in range(0, 512, META):
                factor = weights[at : at + height, start + col : start + col + META]
                dot += value[:, col : col + META] * factor
        dots.append(jnp.sum(dot, axis=1, keepdims=True))
        if packed is not None:
            own = jnp.dot(chosen, meta, preferred_element_type=F32).astype(BF16)
            gates[at : at + height, :] = jnp.dot(own, spread, preferred_element_type=F32)
        at += height
    return dots


def multiply(packed, turned, out):
    units = turned.shape[1]
    for at in range(0, units, TILE):
        size = min(TILE, units - at)
        out[:, at : at + size] = jnp.dot(
            packed[...], turned[:, at : at + size], preferred_element_type=F32
        )


def smem():
    return pl.BlockSpec(memory_space=pltpu.SMEM)


def vmem():
    return pl.BlockSpec(memory_space=pltpu.VMEM)


def anywhere():
    return pl.BlockSpec(memory_space=pl.ANY)


def params(mebibytes=VMEM_LIMIT):
    return pltpu.CompilerParams(vmem_limit_bytes=mebibytes << 20)


def small():
    return pl.CostEstimate(flops=1, bytes_accessed=1, transcendentals=0)


def meta_kernel(place, ids, gates, meta, lines, spot):
    for n in range(4):
        spot[n] = place[n]
    tokens = ids.shape[1]
    expert = lax.broadcasted_iota(jnp.int32, (EXPERTS, tokens), 0)
    named = [ids[k : k + 1, :] == expert for k in range(TOP)]
    some = jnp.zeros((EXPERTS, tokens), F32)
    gate = jnp.zeros((EXPERTS, tokens), F32)
    weights = gates[...].astype(F32)
    for k in range(TOP):
        some = jnp.where(named[k], 1.0, some)
        gate = jnp.where(named[k], weights[k : k + 1, :], gate)
    row = lax.broadcasted_iota(jnp.int32, (tokens, tokens), 0)
    col = lax.broadcasted_iota(jnp.int32, (tokens, tokens), 1)
    earlier = (row < col).astype(F32).astype(BF16)
    before = jnp.dot(some.astype(BF16), earlier, preferred_element_type=F32)
    slot = jnp.where(some > 0.0, before, -1.0)
    lines[...] = jnp.zeros(lines.shape, jnp.int32)
    for k in range(TOP):
        own = jnp.sum(jnp.where(named[k], before, 0.0), axis=0, keepdims=True)
        lines[0:1, k * tokens : (k + 1) * tokens] = (
            own.astype(jnp.int32) + (ids[k : k + 1, :] & 1) * LANES
        )
        lines[1:2, k * tokens : (k + 1) * tokens] = ids[k : k + 1, :]
    table = jnp.concatenate(
        [slot, gate, jnp.zeros((META - 2 * EXPERTS, tokens), F32)], axis=0
    ).astype(BF16)
    unit = (row == col).astype(F32).astype(BF16)
    meta[...] = lax.dot_general(
        unit, table, (((1,), (1,)), ((), ())), preferred_element_type=F32
    ).astype(BF16)


def meta_of(place, ids, gates):
    return pl.pallas_call(
        meta_kernel,
        out_shape=(
            jax.ShapeDtypeStruct((ids.shape[1], META), BF16),
            jax.ShapeDtypeStruct((8, META), jnp.int32),
            jax.ShapeDtypeStruct((4,), jnp.int32),
        ),
        in_specs=[smem(), vmem(), vmem()],
        out_specs=(vmem(), vmem(), smem()),
        compiler_params=params(2),
    )(place, ids, gates)


def join_kernel(*refs):
    at = 0
    for ref in refs[:-1]:
        refs[-1][at : at + ref.shape[0], :] = ref[...]
        at += ref.shape[0]


def join(*parts):
    shape = (sum(p.shape[0] for p in parts), parts[0].shape[1])
    return pl.pallas_call(
        join_kernel,
        out_shape=pltpu.VMEM(shape, parts[0].dtype),
        in_specs=[vmem()] * len(parts),
        out_specs=vmem(),
        compiler_params=params(6),
        cost_estimate=small(),
    )(*parts)


def halves_kernel(high, low, first_half, second_half):
    half = first_half.shape[0]
    first_half[...] = high[:half, :]
    second_half[...] = low[half:, :]


def halves_of(high, low):
    shape = (high.shape[0] // 2, high.shape[1])
    return pl.pallas_call(
        halves_kernel,
        out_shape=(pltpu.VMEM(shape, BF16), pltpu.VMEM(shape, BF16)),
        in_specs=[vmem()] * 2,
        out_specs=(vmem(), vmem()),
        compiler_params=params(6),
        cost_estimate=small(),
    )(high, low)


def far_block(place, n):
    which, a = divmod(n, 4)
    kind = place[2] if which == 0 else 1 - place[2]
    x = jnp.where(kind == 0, OFFSETS[a], 2)
    y = jnp.where(kind == 0, 2, OFFSETS[a])
    return kind, chip_of(place, x, y)


def turn_kernel(place, weight, turned, held, sems):
    units, width = weight.shape
    copies = [
        pltpu.make_async_copy(
            weight.at[pl.ds(at, META), :], held.at[pl.ds(at, META), :], sems.at[at // META]
        )
        for at in range(0, units, META)
    ]
    for copy in copies:
        copy.start()
    for copy, at in zip(copies, range(0, units, META)):
        copy.wait()
        for col in range(0, width, 512):
            turned[col : col + 512, at : at + META] = held[at : at + META, col : col + 512].T


def turn(place, weight):
    units, width = weight.shape
    return pl.pallas_call(
        turn_kernel,
        out_shape=pltpu.VMEM((width, units), BF16),
        in_specs=[smem(), anywhere()],
        out_specs=vmem(),
        scratch_shapes=[
            pltpu.VMEM((units, width), BF16),
            pltpu.SemaphoreType.DMA((units // META,)),
        ],
        compiler_params=params(),
        cost_estimate=small(),
    )(place, pltpu.with_memory_space_constraint(weight, pltpu.HBM))


def ahead_kernel(place, hidden, weight, mine, theirs, held, far, sems):
    units, width = weight.shape
    spans = [pl.ds(at, min(512, units - at)) for at in range(0, units, 512)]
    copies = [
        pltpu.make_async_copy(weight.at[span, :], held.at[span, :], sems.at[n])
        for n, span in enumerate(spans)
    ]
    for copy in copies:
        copy.start()
    for n in range(far.shape[0] // CAP):
        kind, chip = far_block(place, n)
        pair = hidden[pair_rows(chip), :].astype(F32)
        far[n * CAP : (n + 1) * CAP, :] = jnp.where(kind == 0, pair[:CAP], pair[CAP:])
    for n, span in enumerate(spans):
        copies[n].wait()
        at = slice(span.start, span.start + span.size)
        left = far[:, at].astype(BF16)
        for col in range(0, width, 512):
            value = jnp.dot(left, held[at, col : col + 512], preferred_element_type=F32)
            half = mine.shape[0]
            for ref, part in ((mine, value[:half]), (theirs, value[half:])):
                if n:
                    part = ref[:, col : col + 512] + part
                ref[:, col : col + 512] = part


def ahead_of(place, hidden, weight):
    units, width = weight.shape
    height = hidden.shape[0] // 4
    return pl.pallas_call(
        ahead_kernel,
        out_shape=(pltpu.VMEM((height // 2, width), F32),) * 2,
        in_specs=[smem(), vmem(), anywhere()],
        out_specs=(vmem(), vmem()),
        scratch_shapes=[
            pltpu.VMEM((units, width), BF16),
            pltpu.VMEM((height, units), F32),
            pltpu.SemaphoreType.DMA((pl.cdiv(units, 512),)),
        ],
        compiler_params=params(),
        cost_estimate=small(),
    )(place, hidden, pltpu.with_memory_space_constraint(weight, pltpu.HBM))


def near_kernel(place, mine, theirs, turned, out, gates, packed):
    pack(place[3], (mine, theirs), packed, gates)
    multiply(packed, turned, out)


def near_of(place, mine, theirs, turned):
    width, units = turned.shape
    height = 2 * mine.shape[0] // ROWS * CAP
    return pl.pallas_call(
        near_kernel,
        out_shape=(pltpu.VMEM((height, units), F32), pltpu.VMEM((height, META), F32)),
        in_specs=[smem()] + [vmem()] * 3,
        out_specs=(vmem(), vmem()),
        scratch_shapes=[pltpu.VMEM((height, width), BF16)],
        compiler_params=params(),
        cost_estimate=small(),
    )(place, mine, theirs, turned)


def chip_of(place, i, j):
    return ((place[0] + (i + 4)) % 4) * 4 + (place[1] + (j + 4)) % 4


def pair_rows(chip):
    return pl.ds(pl.multiple_of(chip * (2 * CAP), 16), 2 * CAP)


def block_rows(place, kind, group, along):
    which = jnp.where(place[2] == kind, 0, 1)
    return pl.ds(pl.multiple_of((which * group + along) * CAP, 8), CAP)


def diagonal_of(core):
    line = lax.broadcasted_iota(jnp.int32, (CAP, META), 0)
    lane = lax.broadcasted_iota(jnp.int32, (CAP, META), 1)
    return lane == line + core * LANES


def finish(core, chip, pieces, saved, sums, write):
    diagonal = diagonal_of(core)
    scales = [None if p is None or p[1] is None else p[1][p[2], :] for p in pieces]
    totals = [jnp.zeros((CAP, META), F32) for _ in pieces]
    for col in range(0, saved.shape[1], META):
        span = slice(col, col + META)
        factor = saved[pair_rows(chip), span].astype(F32)
        scaled = []
        for kind, piece in enumerate(pieces):
            if piece is None:
                scaled.append(None)
                continue
            value = piece[0][piece[2], span]
            if scales[kind] is not None:
                totals[kind] += factor[kind * CAP : (kind + 1) * CAP] * value
                value = scales[kind] * value
            scaled.append(value)
        write(span, scaled)
    for kind, scale in enumerate(scales):
        if scale is not None:
            total = jnp.sum(totals[kind], axis=1, keepdims=True)
            sums[pl.ds(chip * 2 + kind, 1), :] = jnp.sum(
                jnp.where(diagonal, total, 0.0), axis=0, keepdims=True
            )


def staged(stage, slot):
    def write(span, scaled):
        stage[slot, :, span] = jnp.concatenate(scaled, axis=0).astype(BF16)

    return write


def mid_kernel(
    place, low, high, low_other, high_other, turned, hidden, near, near_gates,
    grad, sums, halves, packed, mid, mid_gates, stage, sems,
):
    sums[...] = jnp.zeros(sums.shape, F32)
    pack(place[3], (low, high, low_other, high_other), packed, mid_gates)
    multiply(packed, turned, mid)

    def piece(kind, along, across):
        a = OFFSETS.index(along)
        if across == 0:
            return near, near_gates, block_rows(place, kind, 4, a)
        return mid, mid_gates, block_rows(place, kind, 8, (0 if across == -1 else 4) + a)

    copies = []
    for i in (0, -1, 1):
        for j in (0, -1, 1):
            chip, slot = chip_of(place, i, j), len(copies)
            pair = piece(0, i, j), piece(1, j, i)
            finish(place[2], chip, pair, hidden, sums, staged(stage, slot))
            copy = pltpu.make_async_copy(stage.at[slot], grad.at[pair_rows(chip), :], sems.at[slot])
            copy.start()
            copies.append(copy)
    for n, (kind, i, j) in enumerate(HALVES):
        def write(span, scaled, kind=kind, n=n):
            halves[n * CAP : (n + 1) * CAP, span] = scaled[kind]

        pieces = (piece(0, i, j), None) if kind == 0 else (None, piece(1, j, i))
        finish(place[2], chip_of(place, i, j), pieces, hidden, sums, write)
    for copy in copies:
        copy.wait()


def mid_of(place, tokens, turned, hidden, near, near_gates):
    width, units = turned.shape
    height = sum(t.shape[0] for t in tokens) // ROWS * CAP
    return pl.pallas_call(
        mid_kernel,
        out_shape=(
            jax.ShapeDtypeStruct(hidden.shape, BF16),
            pltpu.VMEM((hidden.shape[0] // CAP, META), F32),
            pltpu.VMEM((len(HALVES) * CAP, units), F32),
        ),
        in_specs=[smem()] + [vmem()] * 8,
        out_specs=(anywhere(), vmem(), vmem()),
        scratch_shapes=[
            pltpu.VMEM((height, width), BF16),
            pltpu.VMEM((height, units), F32),
            pltpu.VMEM((height, META), F32),
            pltpu.VMEM((9, 2 * CAP, units), BF16),
            pltpu.SemaphoreType.DMA((9,)),
        ],
        compiler_params=params(),
        cost_estimate=small(),
    )(place, *tokens, turned, hidden, near, near_gates)


def sums_kernel(place, tokens, ahead, other_ahead, early, sums, packed, gates):
    sums[...] = early[...]
    core = place[2]
    (total,) = pack(place[3], (tokens,), packed, gates, ahead)
    (other,) = pack(place[3] + 1 - 2 * core, (tokens,), None, None, other_ahead)
    diagonal, other_diagonal = diagonal_of(core), diagonal_of(1 - core)
    for n in range(4):
        kind, chip = far_block(place, n)
        block = slice(n * CAP, (n + 1) * CAP)
        line = jnp.where(diagonal, total[block], jnp.where(other_diagonal, other[block], 0.0))
        sums[pl.ds(chip * 2 + kind, 1), :] = jnp.sum(line, axis=0, keepdims=True)


def sums_of(place, tokens, ahead, other_ahead, early):
    height, width = ahead.shape
    return pl.pallas_call(
        sums_kernel,
        out_shape=(
            pltpu.VMEM(early.shape, F32),
            pltpu.VMEM((height, width), BF16),
            pltpu.VMEM((height, META), F32),
        ),
        in_specs=[smem()] + [vmem()] * 4,
        out_specs=(vmem(), vmem(), vmem()),
        compiler_params=params(),
        cost_estimate=small(),
    )(place, tokens, ahead, other_ahead, early)


def far_kernel(
    place, mine, gates, tokens, turned, halves, _, grad,
    held, theirs, other_gates, far, far_scales, stage, sems, loads,
):
    units = far.shape[1]
    spans = [pl.ds(at, 512) for at in range(0, held.shape[0], 512)]
    copies = [
        pltpu.make_async_copy(turned.at[span, :], held.at[span, :], loads.at[n])
        for n, span in enumerate(spans)
    ]
    for copy in copies:
        copy.start()
    pack(place[3], (tokens,), theirs, other_gates)
    for n, span in enumerate(spans):
        copies[n].wait()
        at = slice(span.start, span.start + span.size)
        rows_of = jnp.concatenate([mine[:, at], theirs[:, at]], axis=0)
        value = jnp.dot(rows_of, held[at, :], preferred_element_type=F32)
        far[...] = value if n == 0 else far[...] + value
    copies = []
    scales = jnp.concatenate([gates[...], other_gates[...]], axis=0)
    far_scales[...] = scales
    for i in OFFSETS:
        for j in OFFSETS:
            if i != 2 and j != 2:
                continue
            pieces = []
            for kind, along, across in ((0, i, j), (1, j, i)):
                if across == 2:
                    span = block_rows(place, kind, 4, OFFSETS.index(along))
                    pieces.append((far, far_scales[span, :], span))
                else:
                    n = HALVES.index((kind, i, j))
                    pieces.append((halves, None, pl.ds(n * CAP, CAP)))
            chip, slot = chip_of(place, i, j), len(copies)
            for col in range(0, units, META):
                span = slice(col, col + META)
                scaled = [
                    ref[at, span] if scale is None else scale * ref[at, span]
                    for ref, scale, at in pieces
                ]
                stage[slot, :, span] = jnp.concatenate(scaled, axis=0).astype(BF16)
            copy = pltpu.make_async_copy(stage.at[slot], grad.at[pair_rows(chip), :], sems.at[slot])
            copy.start()
            copies.append(copy)
    for copy in copies:
        copy.wait()


def far_of(place, mine, gates, tokens, turned, halves, grad):
    width, units = turned.shape
    height = 2 * mine.shape[0]
    return pl.pallas_call(
        far_kernel,
        out_shape=jax.ShapeDtypeStruct(grad.shape, BF16),
        in_specs=[smem()] + [vmem()] * 3 + [anywhere(), vmem(), anywhere()],
        out_specs=anywhere(),
        scratch_shapes=[
            pltpu.VMEM((width, units), BF16),
            pltpu.VMEM((height // 2, width), BF16),
            pltpu.VMEM((height // 2, META), F32),
            pltpu.VMEM((height, units), F32),
            pltpu.VMEM((height, META), F32),
            pltpu.VMEM((7, 2 * CAP, units), BF16),
            pltpu.SemaphoreType.DMA((7,)),
            pltpu.SemaphoreType.DMA((width // 512,)),
        ],
        input_output_aliases={6: 0},
        compiler_params=params(),
        cost_estimate=pl.CostEstimate(
            flops=2 * height * units * turned.shape[0], bytes_accessed=1, transcendentals=0
        ),
    )(
        place, mine, gates, tokens,
        pltpu.with_memory_space_constraint(turned, pltpu.HBM), halves, grad,
    )


def gather_kernel(totals, lines, out):
    quarter = totals.shape[0] // 4
    total = totals[0:quarter, :]
    for n in range(1, 4):
        total = total + totals[n * quarter : (n + 1) * quarter, :]
    pick = (lax.broadcasted_iota(jnp.int32, (META, META), 0) == lines[0:1, :]).astype(F32)
    line = jnp.dot(total, pick, precision=lax.Precision.HIGHEST, preferred_element_type=F32)
    chosen = (lax.broadcasted_iota(jnp.int32, line.shape, 0) >> 1) == (lines[1:2, :] >> 1)
    line = jnp.sum(jnp.where(chosen, line, 0.0), axis=0, keepdims=True)
    tokens = out.shape[1]
    for k in range(TOP):
        out[k : k + 1, :] = line[:, k * tokens : (k + 1) * tokens]


def on_device(handoff, expert_ids, gates, down_weight, hidden):
    dp, expert = lax.axis_index("dp"), lax.axis_index("expert")
    place = jnp.stack([dp, expert // 2, expert % 2, expert]).astype(jnp.int32)
    ids = expert_ids[0].T
    weight, saved = down_weight[0, 0], hidden[0, 0]
    incoming = moved(handoff[0], previous_section)
    meta, lines, place = meta_of(place, ids, gates[0].T)
    incoming, meta, lines, place = lax.optimization_barrier((incoming, meta, lines, place))
    own = jnp.concatenate([incoming, meta], axis=1)
    own, place = lax.optimization_barrier((own, place))

    ahead, back, across = [moved(own, first(k)) for k in (1, 3, 2)]
    turned = turn(place, weight)
    ahead, back, across, turned = lax.optimization_barrier((ahead, back, across, turned))
    near = rows(own, ahead, back, across)
    low, high = moved(near, second(1)), moved(near, second(3))
    near_other = moved(near, other_core)
    near_other, later = lax.optimization_barrier((near_other, place))
    near_done = near_of(place, near, near_other, turned)
    ahead_far, ahead_other = ahead_of(later, saved, weight)
    low, high, ahead_far, ahead_other, *near_done = lax.optimization_barrier(
        (low, high, ahead_far, ahead_other, *near_done)
    )
    ahead_other = moved(ahead_other, other_core)
    left, right = halves_of(high, low)
    far = moved(left, second(3)), moved(right, second(1))
    tokens = low, high, moved(low, other_core), moved(high, other_core)
    grad, sums, halves = mid_of(place, tokens, turned, saved, *near_done)
    *far, grad, sums, halves = lax.optimization_barrier((*far, grad, sums, halves))
    far = join(*far)
    far_other = moved(far, other_core)
    sums, mine, far_gates = sums_of(place, far, ahead_far, ahead_other, sums)
    sums, far_other = lax.optimization_barrier((sums, far_other))
    totals = lax.all_to_all(sums, ("dp", "expert"), split_axis=0, concat_axis=0, tiled=True)
    grad = far_of(place, mine, far_gates, far_other, turned, halves, grad)
    gate_grad = pl.pallas_call(
        gather_kernel,
        out_shape=jax.ShapeDtypeStruct(ids.shape, F32),
        in_specs=[vmem()] * 2,
        out_specs=vmem(),
        compiler_params=params(2),
    )(totals, lines)
    return (grad[None, None], gate_grad.T[None])


def solution(mesh):
    return jax.shard_map(
        on_device,
        mesh=mesh,
        in_specs=(
            P("pipe", ("dp", "expert"), None),
            P("pipe", ("dp", "expert"), None),
            P("pipe", ("dp", "expert"), None),
            P("pipe", "expert", "dp", None),
            P("pipe", "expert", None, "dp"),
        ),
        out_specs=(P("pipe", "expert", None, "dp"), P("pipe", ("dp", "expert"), None)),
        check_vma=False,
    )
```

```python
import jax
import jax.numpy as jnp
from jax import lax
from jax.experimental import pallas as pl
from jax.experimental.pallas import tpu as pltpu
from jax.sharding import PartitionSpec as P

EXPERTS = 8
TOP = 4
CAP = 24
ROWS = 32
META = 128
LANES = 32
TILE = 256
OFFSETS = (0, -1, 1, 2)
HALVES = tuple((0, 2, j) for j in (0, -1, 1)) + tuple((1, i, 2) for i in (0, -1, 1))
AXES = ("pipe", "dp", "expert")
VMEM_LIMIT = 20
F32 = jnp.float32
BF16 = jnp.bfloat16


def moved(x, to):
    nz, nx, ne = (lax.axis_size(a) for a in AXES)
    ny = ne // 2

    def index(z, i, j, c):
        return ((z % nz) * nx + i % nx) * ne + (j % ny) * 2 + c

    pairs = [
        (index(z, i, j, c), index(*to(z, i, j, c)))
        for z in range(nz)
        for i in range(nx)
        for j in range(ny)
        for c in range(2)
    ]
    return lax.ppermute(x, AXES, pairs)


def first(k):
    return lambda z, i, j, c: (z, i + k, j, c) if c == 0 else (z, i, j + k, c)


def second(k):
    return lambda z, i, j, c: (z, i, j + k, c) if c == 0 else (z, i + k, j, c)


def other_core(z, i, j, c):
    return (z, i, j, 1 - c)


def previous_section(z, i, j, c):
    return (z - 1, i, j, c)


def rows(*parts):
    return jnp.concatenate(parts, axis=0)


def chosen_rows(expert, ref):
    count, width = ref.shape
    lane = lax.broadcasted_iota(jnp.int32, (16, META), 1)
    line = lax.broadcasted_iota(jnp.int32, (16, META), 0)
    pick = ((line == 0) & (lane == expert)).astype(F32).astype(BF16)
    slot = lax.dot_general(
        pick, ref[:, width - META :], (((1,), (1,)), ((), ())), preferred_element_type=F32
    )[0:1, :]
    block = lax.broadcasted_iota(jnp.int32, (1, count), 1) // ROWS
    target = jnp.where(slot >= 0.0, slot.astype(jnp.int32) + block * CAP, -1)
    place = lax.broadcasted_iota(jnp.int32, (count // ROWS * CAP, count), 0)
    return (place == target).astype(F32).astype(BF16)


def pack(expert, token_refs, packed, gates):
    spread = (
        lax.broadcasted_iota(jnp.int32, (META, META), 0) == EXPERTS + expert
    ).astype(F32).astype(BF16)
    at = 0
    for ref in token_refs:
        width = ref.shape[1] - META
        chosen = chosen_rows(expert, ref)
        height = chosen.shape[0]
        for start in range(0, width, 512):
            packed[at : at + height, start : start + 512] = jnp.dot(
                chosen, ref[:, start : start + 512], preferred_element_type=F32
            ).astype(BF16)
        own = jnp.dot(chosen, ref[:, width:], preferred_element_type=F32).astype(BF16)
        gates[at : at + height, :] = jnp.dot(own, spread, preferred_element_type=F32)
        at += height


def multiply(packed, turned, out):
    units = turned.shape[1]
    for at in range(0, units, TILE):
        size = min(TILE, units - at)
        out[:, at : at + size] = jnp.dot(
            packed[...], turned[:, at : at + size], preferred_element_type=F32
        )


def smem():
    return pl.BlockSpec(memory_space=pltpu.SMEM)


def vmem():
    return pl.BlockSpec(memory_space=pltpu.VMEM)


def anywhere():
    return pl.BlockSpec(memory_space=pl.ANY)


def params(mebibytes=VMEM_LIMIT):
    return pltpu.CompilerParams(vmem_limit_bytes=mebibytes << 20)


def small():
    return pl.CostEstimate(flops=1, bytes_accessed=1, transcendentals=0)


def meta_kernel(place, ids, gates, meta, lines, spot):
    for n in range(4):
        spot[n] = place[n]
    tokens = ids.shape[1]
    expert = lax.broadcasted_iota(jnp.int32, (EXPERTS, tokens), 0)
    named = [ids[k : k + 1, :] == expert for k in range(TOP)]
    some = jnp.zeros((EXPERTS, tokens), F32)
    gate = jnp.zeros((EXPERTS, tokens), F32)
    weights = gates[...].astype(F32)
    for k in range(TOP):
        some = jnp.where(named[k], 1.0, some)
        gate = jnp.where(named[k], weights[k : k + 1, :], gate)
    row = lax.broadcasted_iota(jnp.int32, (tokens, tokens), 0)
    col = lax.broadcasted_iota(jnp.int32, (tokens, tokens), 1)
    earlier = (row < col).astype(F32).astype(BF16)
    before = jnp.dot(some.astype(BF16), earlier, preferred_element_type=F32)
    slot = jnp.where(some > 0.0, before, -1.0)
    lines[...] = jnp.zeros(lines.shape, jnp.int32)
    for k in range(TOP):
        own = jnp.sum(jnp.where(named[k], before, 0.0), axis=0, keepdims=True)
        lines[0:1, k * tokens : (k + 1) * tokens] = (
            own.astype(jnp.int32) + (ids[k : k + 1, :] & 1) * LANES
        )
        lines[1:2, k * tokens : (k + 1) * tokens] = ids[k : k + 1, :]
    table = jnp.concatenate(
        [slot, gate, jnp.zeros((META - 2 * EXPERTS, tokens), F32)], axis=0
    ).astype(BF16)
    unit = (row == col).astype(F32).astype(BF16)
    meta[...] = lax.dot_general(
        unit, table, (((1,), (1,)), ((), ())), preferred_element_type=F32
    ).astype(BF16)


def meta_of(place, ids, gates):
    return pl.pallas_call(
        meta_kernel,
        out_shape=(
            jax.ShapeDtypeStruct((ids.shape[1], META), BF16),
            jax.ShapeDtypeStruct((8, META), jnp.int32),
            jax.ShapeDtypeStruct((4,), jnp.int32),
        ),
        in_specs=[smem(), vmem(), vmem()],
        out_specs=(vmem(), vmem(), smem()),
        compiler_params=params(2),
    )(place, ids, gates)


def join_kernel(*refs):
    at = 0
    for ref in refs[:-1]:
        refs[-1][at : at + ref.shape[0], :] = ref[...]
        at += ref.shape[0]


def join(*parts):
    shape = (sum(p.shape[0] for p in parts), parts[0].shape[1])
    return pl.pallas_call(
        join_kernel,
        out_shape=pltpu.VMEM(shape, parts[0].dtype),
        in_specs=[vmem()] * len(parts),
        out_specs=vmem(),
        compiler_params=params(6),
        cost_estimate=small(),
    )(*parts)


def halves_kernel(high, low, first_half, second_half):
    half = first_half.shape[0]
    first_half[...] = high[:half, :]
    second_half[...] = low[half:, :]


def halves_of(high, low):
    shape = (high.shape[0] // 2, high.shape[1])
    return pl.pallas_call(
        halves_kernel,
        out_shape=(pltpu.VMEM(shape, BF16), pltpu.VMEM(shape, BF16)),
        in_specs=[vmem()] * 2,
        out_specs=(vmem(), vmem()),
        compiler_params=params(6),
        cost_estimate=small(),
    )(high, low)


def far_block(place, n):
    which, a = divmod(n, 4)
    kind = place[2] if which == 0 else 1 - place[2]
    x = jnp.where(kind == 0, OFFSETS[a], 2)
    y = jnp.where(kind == 0, 2, OFFSETS[a])
    return kind, chip_of(place, x, y)


def turn_kernel(place, weight, turned, held, sems):
    units, width = weight.shape
    copies = [
        pltpu.make_async_copy(
            weight.at[pl.ds(at, META), :], held.at[pl.ds(at, META), :], sems.at[at // META]
        )
        for at in range(0, units, META)
    ]
    for copy in copies:
        copy.start()
    for copy, at in zip(copies, range(0, units, META)):
        copy.wait()
        for col in range(0, width, 512):
            turned[col : col + 512, at : at + META] = held[at : at + META, col : col + 512].T


def turn(place, weight):
    units, width = weight.shape
    return pl.pallas_call(
        turn_kernel,
        out_shape=pltpu.VMEM((width, units), BF16),
        in_specs=[smem(), anywhere()],
        out_specs=vmem(),
        scratch_shapes=[
            pltpu.VMEM((units, width), BF16),
            pltpu.SemaphoreType.DMA((units // META,)),
        ],
        compiler_params=params(),
        cost_estimate=small(),
    )(place, pltpu.with_memory_space_constraint(weight, pltpu.HBM))


def ahead_kernel(place, hidden, weight, mine, theirs, held, far, sems):
    units, width = weight.shape
    spans = [pl.ds(at, min(512, units - at)) for at in range(0, units, 512)]
    copies = [
        pltpu.make_async_copy(weight.at[span, :], held.at[span, :], sems.at[n])
        for n, span in enumerate(spans)
    ]
    for copy in copies:
        copy.start()
    for n in range(far.shape[0] // CAP):
        kind, chip = far_block(place, n)
        pair = hidden[pair_rows(chip), :].astype(F32)
        far[n * CAP : (n + 1) * CAP, :] = jnp.where(kind == 0, pair[:CAP], pair[CAP:])
    for n, span in enumerate(spans):
        copies[n].wait()
        at = slice(span.start, span.start + span.size)
        left = far[:, at].astype(BF16)
        for col in range(0, width, 512):
            value = jnp.dot(left, held[at, col : col + 512], preferred_element_type=F32)
            half = mine.shape[0]
            for ref, part in ((mine, value[:half]), (theirs, value[half:])):
                if n:
                    part = ref[:, col : col + 512] + part
                ref[:, col : col + 512] = part


def ahead_of(place, hidden, weight):
    units, width = weight.shape
    height = hidden.shape[0] // 4
    return pl.pallas_call(
        ahead_kernel,
        out_shape=(pltpu.VMEM((height // 2, width), F32),) * 2,
        in_specs=[smem(), vmem(), anywhere()],
        out_specs=(vmem(), vmem()),
        scratch_shapes=[
            pltpu.VMEM((units, width), BF16),
            pltpu.VMEM((height, units), F32),
            pltpu.SemaphoreType.DMA((pl.cdiv(units, 512),)),
        ],
        compiler_params=params(),
        cost_estimate=small(),
    )(place, hidden, pltpu.with_memory_space_constraint(weight, pltpu.HBM))


def near_kernel(place, mine, theirs, turned, out, gates, packed):
    pack(place[3], (mine, theirs), packed, gates)
    multiply(packed, turned, out)


def near_of(place, mine, theirs, turned):
    width, units = turned.shape
    height = 2 * mine.shape[0] // ROWS * CAP
    return pl.pallas_call(
        near_kernel,
        out_shape=(pltpu.VMEM((height, units), F32), pltpu.VMEM((height, META), F32)),
        in_specs=[smem()] + [vmem()] * 3,
        out_specs=(vmem(), vmem()),
        scratch_shapes=[pltpu.VMEM((height, width), BF16)],
        compiler_params=params(),
        cost_estimate=small(),
    )(place, mine, theirs, turned)


def chip_of(place, i, j):
    return ((place[0] + (i + 4)) % 4) * 4 + (place[1] + (j + 4)) % 4


def pair_rows(chip):
    return pl.ds(pl.multiple_of(chip * (2 * CAP), 16), 2 * CAP)


def block_rows(place, kind, group, along):
    which = jnp.where(place[2] == kind, 0, 1)
    return pl.ds(pl.multiple_of((which * group + along) * CAP, 8), CAP)


def diagonal_of(core):
    line = lax.broadcasted_iota(jnp.int32, (CAP, META), 0)
    lane = lax.broadcasted_iota(jnp.int32, (CAP, META), 1)
    return lane == line + core * LANES


def finish(core, chip, pieces, saved, sums, write):
    diagonal = diagonal_of(core)
    scales = [None if p is None or p[1] is None else p[1][p[2], :] for p in pieces]
    totals = [jnp.zeros((CAP, META), F32) for _ in pieces]
    for col in range(0, saved.shape[1], META):
        span = slice(col, col + META)
        factor = saved[pair_rows(chip), span].astype(F32)
        scaled = []
        for kind, piece in enumerate(pieces):
            if piece is None:
                scaled.append(None)
                continue
            value = piece[0][piece[2], span]
            if scales[kind] is not None:
                totals[kind] += factor[kind * CAP : (kind + 1) * CAP] * value
                value = scales[kind] * value
            scaled.append(value)
        write(span, scaled)
    for kind, scale in enumerate(scales):
        if scale is not None:
            total = jnp.sum(totals[kind], axis=1, keepdims=True)
            sums[pl.ds(chip * 2 + kind, 1), :] = jnp.sum(
                jnp.where(diagonal, total, 0.0), axis=0, keepdims=True
            )


def staged(stage, slot):
    def write(span, scaled):
        stage[slot, :, span] = jnp.concatenate(scaled, axis=0).astype(BF16)

    return write


def mid_kernel(
    place, low, high, low_other, high_other, turned, hidden, near, near_gates,
    grad, sums, halves, packed, mid, mid_gates, stage, sems,
):
    sums[...] = jnp.zeros(sums.shape, F32)
    pack(place[3], (low, high, low_other, high_other), packed, mid_gates)
    multiply(packed, turned, mid)

    def piece(kind, along, across):
        a = OFFSETS.index(along)
        if across == 0:
            return near, near_gates, block_rows(place, kind, 4, a)
        return mid, mid_gates, block_rows(place, kind, 8, (0 if across == -1 else 4) + a)

    copies = []
    for i in (0, -1, 1):
        for j in (0, -1, 1):
            chip, slot = chip_of(place, i, j), len(copies)
            pair = piece(0, i, j), piece(1, j, i)
            finish(place[2], chip, pair, hidden, sums, staged(stage, slot))
            copy = pltpu.make_async_copy(stage.at[slot], grad.at[pair_rows(chip), :], sems.at[slot])
            copy.start()
            copies.append(copy)
    for n, (kind, i, j) in enumerate(HALVES):
        def write(span, scaled, kind=kind, n=n):
            halves[n * CAP : (n + 1) * CAP, span] = scaled[kind]

        pieces = (piece(0, i, j), None) if kind == 0 else (None, piece(1, j, i))
        finish(place[2], chip_of(place, i, j), pieces, hidden, sums, write)
    for copy in copies:
        copy.wait()


def mid_of(place, tokens, turned, hidden, near, near_gates):
    width, units = turned.shape
    height = sum(t.shape[0] for t in tokens) // ROWS * CAP
    return pl.pallas_call(
        mid_kernel,
        out_shape=(
            jax.ShapeDtypeStruct(hidden.shape, BF16),
            pltpu.VMEM((hidden.shape[0] // CAP, META), F32),
            pltpu.VMEM((len(HALVES) * CAP, units), F32),
        ),
        in_specs=[smem()] + [vmem()] * 8,
        out_specs=(anywhere(), vmem(), vmem()),
        scratch_shapes=[
            pltpu.VMEM((height, width), BF16),
            pltpu.VMEM((height, units), F32),
            pltpu.VMEM((height, META), F32),
            pltpu.VMEM((9, 2 * CAP, units), BF16),
            pltpu.SemaphoreType.DMA((9,)),
        ],
        compiler_params=params(),
        cost_estimate=small(),
    )(place, *tokens, turned, hidden, near, near_gates)


def sums_kernel(place, tokens, ahead, other_ahead, early, sums):
    sums[...] = early[...]
    core = place[2]
    height, width = ahead.shape
    chosen = jnp.concatenate(
        [chosen_rows(e, tokens) for e in (place[3], place[3] + 1 - 2 * core)], axis=0
    )
    total = jnp.zeros((2 * height, META), F32)
    for start in range(0, width, 512):
        value = jnp.dot(chosen, tokens[:, start : start + 512], preferred_element_type=F32)
        for col in range(0, 512, META):
            span = slice(start + col, start + col + META)
            factor = jnp.concatenate([ahead[:, span], other_ahead[:, span]], axis=0)
            total += value[:, col : col + META] * factor
    total = jnp.sum(total, axis=1, keepdims=True)
    diagonal, other_diagonal = diagonal_of(core), diagonal_of(1 - core)
    for n in range(4):
        kind, chip = far_block(place, n)
        own = total[n * CAP : (n + 1) * CAP]
        other = total[height + n * CAP : height + (n + 1) * CAP]
        line = jnp.where(diagonal, own, jnp.where(other_diagonal, other, 0.0))
        sums[pl.ds(chip * 2 + kind, 1), :] = jnp.sum(line, axis=0, keepdims=True)


def sums_of(place, tokens, ahead, other_ahead, early):
    return pl.pallas_call(
        sums_kernel,
        out_shape=jax.ShapeDtypeStruct(early.shape, F32),
        in_specs=[smem()] + [vmem()] * 4,
        out_specs=vmem(),
        compiler_params=params(),
        cost_estimate=small(),
    )(place, tokens, ahead, other_ahead, early)


def far_kernel(
    place, mine, theirs, turned, halves, _, grad, held, packed, far, far_scales, stage, sems, loads
):
    units = far.shape[1]
    spans = [pl.ds(at, 512) for at in range(0, held.shape[0], 512)]
    copies = [
        pltpu.make_async_copy(turned.at[span, :], held.at[span, :], loads.at[n])
        for n, span in enumerate(spans)
    ]
    for copy in copies:
        copy.start()
    pack(place[3], (mine, theirs), packed, far_scales)
    for n, span in enumerate(spans):
        copies[n].wait()
        at = slice(span.start, span.start + span.size)
        value = jnp.dot(packed[:, at], held[at, :], preferred_element_type=F32)
        far[...] = value if n == 0 else far[...] + value
    copies = []
    for i in OFFSETS:
        for j in OFFSETS:
            if i != 2 and j != 2:
                continue
            pieces = []
            for kind, along, across in ((0, i, j), (1, j, i)):
                if across == 2:
                    span = block_rows(place, kind, 4, OFFSETS.index(along))
                    pieces.append((far, far_scales[span, :], span))
                else:
                    n = HALVES.index((kind, i, j))
                    pieces.append((halves, None, pl.ds(n * CAP, CAP)))
            chip, slot = chip_of(place, i, j), len(copies)
            for col in range(0, units, META):
                span = slice(col, col + META)
                scaled = [
                    ref[at, span] if scale is None else scale * ref[at, span]
                    for ref, scale, at in pieces
                ]
                stage[slot, :, span] = jnp.concatenate(scaled, axis=0).astype(BF16)
            copy = pltpu.make_async_copy(stage.at[slot], grad.at[pair_rows(chip), :], sems.at[slot])
            copy.start()
            copies.append(copy)
    for copy in copies:
        copy.wait()


def far_of(place, mine, theirs, turned, halves, grad):
    width, units = turned.shape
    height = 2 * mine.shape[0] // ROWS * CAP
    return pl.pallas_call(
        far_kernel,
        out_shape=jax.ShapeDtypeStruct(grad.shape, BF16),
        in_specs=[smem()] + [vmem()] * 2 + [anywhere(), vmem(), anywhere()],
        out_specs=anywhere(),
        scratch_shapes=[
            pltpu.VMEM((width, units), BF16),
            pltpu.VMEM((height, width), BF16),
            pltpu.VMEM((height, units), F32),
            pltpu.VMEM((height, META), F32),
            pltpu.VMEM((7, 2 * CAP, units), BF16),
            pltpu.SemaphoreType.DMA((7,)),
            pltpu.SemaphoreType.DMA((width // 512,)),
        ],
        input_output_aliases={5: 0},
        compiler_params=params(),
        cost_estimate=pl.CostEstimate(
            flops=2 * height * units * turned.shape[0], bytes_accessed=1, transcendentals=0
        ),
    )(
        place, mine, theirs,
        pltpu.with_memory_space_constraint(turned, pltpu.HBM), halves, grad,
    )


def gather_kernel(totals, lines, out):
    quarter = totals.shape[0] // 4
    total = totals[0:quarter, :]
    for n in range(1, 4):
        total = total + totals[n * quarter : (n + 1) * quarter, :]
    pick = (lax.broadcasted_iota(jnp.int32, (META, META), 0) == lines[0:1, :]).astype(F32)
    line = jnp.dot(total, pick, precision=lax.Precision.HIGHEST, preferred_element_type=F32)
    chosen = (lax.broadcasted_iota(jnp.int32, line.shape, 0) >> 1) == (lines[1:2, :] >> 1)
    line = jnp.sum(jnp.where(chosen, line, 0.0), axis=0, keepdims=True)
    tokens = out.shape[1]
    for k in range(TOP):
        out[k : k + 1, :] = line[:, k * tokens : (k + 1) * tokens]


def on_device(handoff, expert_ids, gates, down_weight, hidden):
    dp, expert = lax.axis_index("dp"), lax.axis_index("expert")
    place = jnp.stack([dp, expert // 2, expert % 2, expert]).astype(jnp.int32)
    ids = expert_ids[0].T
    weight, saved = down_weight[0, 0], hidden[0, 0]
    incoming = moved(handoff[0], previous_section)
    meta, lines, place = meta_of(place, ids, gates[0].T)
    incoming, meta, lines, place = lax.optimization_barrier((incoming, meta, lines, place))
    own = jnp.concatenate([incoming, meta], axis=1)
    own, place = lax.optimization_barrier((own, place))

    ahead, back, across = [moved(own, first(k)) for k in (1, 3, 2)]
    turned = turn(place, weight)
    ahead, back, across, turned = lax.optimization_barrier((ahead, back, across, turned))
    near = rows(own, ahead, back, across)
    low, high = moved(near, second(1)), moved(near, second(3))
    near_other = moved(near, other_core)
    near_other, later = lax.optimization_barrier((near_other, place))
    near_done = near_of(place, near, near_other, turned)
    ahead_far, ahead_other = ahead_of(later, saved, weight)
    low, high, ahead_far, ahead_other, *near_done = lax.optimization_barrier(
        (low, high, ahead_far, ahead_other, *near_done)
    )
    ahead_other = moved(ahead_other, other_core)
    left, right = halves_of(high, low)
    far = moved(left, second(3)), moved(right, second(1))
    tokens = low, high, moved(low, other_core), moved(high, other_core)
    grad, sums, halves = mid_of(place, tokens, turned, saved, *near_done)
    *far, grad, sums, halves = lax.optimization_barrier((*far, grad, sums, halves))
    far = join(*far)
    far_other = moved(far, other_core)
    sums = sums_of(place, far, ahead_far, ahead_other, sums)
    totals = lax.all_to_all(sums, ("dp", "expert"), split_axis=0, concat_axis=0, tiled=True)
    grad = far_of(place, far, far_other, turned, halves, grad)
    totals, grad = lax.optimization_barrier((totals, grad))
    gate_grad = pl.pallas_call(
        gather_kernel,
        out_shape=jax.ShapeDtypeStruct(ids.shape, F32),
        in_specs=[vmem()] * 2,
        out_specs=vmem(),
        compiler_params=params(2),
    )(totals, lines)
    return (grad[None, None], gate_grad.T[None])


def solution(mesh):
    return jax.shard_map(
        on_device,
        mesh=mesh,
        in_specs=(
            P("pipe", ("dp", "expert"), None),
            P("pipe", ("dp", "expert"), None),
            P("pipe", ("dp", "expert"), None),
            P("pipe", "expert", "dp", None),
            P("pipe", "expert", None, "dp"),
        ),
        out_specs=(P("pipe", "expert", None, "dp"), P("pipe", ("dp", "expert"), None)),
        check_vma=False,
    )
```
